128 devices in a mesh: sub: 2 (over x_hi), row: 8 (over y, core), col: 8 (over x_lo, z).
Axes of the slice: x: 4 (x_hi: 2, x_lo: 2; x = x_hi * 2 + x_lo), y: 4, z: 4, core: 2. Of those that a mesh axis runs over, the one named last changes fastest.
Arguments:
- child_fronts: float32 [2, 8192, 8192], P('sub', 'row', 'col'), as said below
- child_map: int32 [2, 56], replicated, may hold values from 0 to 95, as said below
- parent_front: float32 [12288, 12288], P(('sub', 'row'), 'col'), as said below
Outputs:
- child_factor: float32 [2, 8192, 1024], P('sub', 'row', 'col')
- parent_factor: float32 [12288, 1024], P(('sub', 'row'), 'col')
- parent_update: float32 [12288, 12288], P(('sub', 'row'), 'col')
The draws below stay inside these ranges and needn't reach their ends.
Inputs may be any that keep to these rules, and one draw needn't show every extreme that they name: The kept blocks of child c are numbered a = 0 .. 55 in increasing order; child_map[c, a] is the parent block that receives kept block a. A child's entries are distinct. Within each run of 7 entries of one child that starts at a multiple of that length, the values child_map // 12 are distinct; for children 2h and 2h + 1 and the same run, the 2 * (7) values child_map // 6 are distinct. `child_fronts`: each front is symmetric with smallest eigenvalue above 0.05. `parent_front`: symmetric with smallest eigenvalue above 0.05.
All inputs are finite; a program needn't handle non-finite values.
Results may differ from the reference program's by a relative error of at most 0.0003.
Values sent between devices are 32-bit elements; how exact they have to be, the bound alone decides.
No kernel may reach another device: no remote copies, remote signals or barrier semaphores. Data moves between devices by JAX's collectives and lax.ppermute only.
A program may use at most 192 MiB of HBM per device.

```python
import math
import jax
import jax.numpy as jnp
import numpy as np
from jax import lax

TILE = 128
STEPS = 8
CBLK = 64
PBLK = 96
CHILDREN = 2
CHILD_ORDER = 8192
PARENT_ORDER = 12288
KEPT = 56


coupling = 0.6


reach = 8.0


def symmetric_front(key, count, order):
    key_noise, key_diag = jax.random.split(key, 2)
    noise = jax.random.normal(key_noise, (count, order, order), jnp.float32)
    front = (noise + jnp.swapaxes(noise, 1, 2)) * (0.6 / math.sqrt(2.0 * order))
    where = jnp.arange(order, dtype=jnp.float32)
    distance = jnp.abs(where[:, None] - where[None, :])
    front = front + (coupling * jnp.exp(-distance / reach))[None, :, :]
    diag = jax.random.uniform(key_diag, (count, order), jnp.float32, 1.6, 3.6)
    place = jnp.arange(order)
    front = front.at[:, place, place].add(diag)
    return front


def draw_child_fronts(key, part):
    return symmetric_front(jax.random.fold_in(key, 11), CHILDREN, CHILD_ORDER)


def draw_parent_front(key, part):
    return symmetric_front(jax.random.fold_in(key, 23), 1, PARENT_ORDER)[0]


def draw_child_map(key, part):
    pairs = CHILDREN // 2
    keep = CBLK // STEPS - 1
    spacing = PBLK // STEPS
    half = spacing // 2
    key_first, key_second, key_offset = jax.random.split(jax.random.fold_in(key, 37), 3)
    first = jax.vmap(lambda k: jax.random.permutation(k, STEPS)[:keep])(jax.random.split(key_first, pairs * STEPS))
    second = jax.vmap(lambda k: jax.random.permutation(k, STEPS)[:keep])(jax.random.split(key_second, pairs * STEPS))
    first = first.reshape(pairs, STEPS, keep)
    second = second.reshape(pairs, STEPS, keep)
    offset = jax.vmap(lambda k: jax.random.permutation(k, spacing)[:STEPS])(jax.random.split(key_offset, pairs))
    upper = offset // half
    lower_part = offset % half
    map_first = first * spacing + (half * upper + lower_part)[:, :, None]
    map_second = second * spacing + (half * (1 - upper) + lower_part)[:, :, None]
    joined = jnp.stack([map_first, map_second], axis=1)
    return joined.reshape(CHILDREN, STEPS * keep).astype(jnp.int32)


def setup_inputs(seed: int = 0) -> dict:
    key_of = jax.random.split(jax.random.key(seed), 4)
    return {
        "child_fronts": draw_child_fronts(jax.random.fold_in(key_of[3], 71), 0),
        "child_map": draw_child_map(jax.random.fold_in(key_of[3], 71), 0),
        "parent_front": draw_parent_front(jax.random.fold_in(key_of[3], 71), 0),
    }


HIGH = lax.Precision.HIGHEST

def split_indices(blocks, spacing):
    pivots = np.concatenate([np.arange(b * TILE, (b + 1) * TILE) for b in range(blocks) if b % spacing == 0])
    kept = np.concatenate([np.arange(b * TILE, (b + 1) * TILE) for b in range(blocks) if b % spacing != 0])
    return (pivots.astype(np.int32), kept.astype(np.int32))

def partial_factor(front, blocks, spacing):
    pivots, kept = split_indices(blocks, spacing)
    top = front[pivots[:, None], pivots[None, :]]
    side = front[kept[:, None], pivots[None, :]]
    lower = jnp.linalg.cholesky(top)
    side_factor = jax.scipy.linalg.solve_triangular(lower, side.T, lower=True).T
    schur = front[kept[:, None], kept[None, :]] - jnp.dot(side_factor, side_factor.T, precision=HIGH)
    factor = jnp.zeros((front.shape[0], pivots.shape[0]), jnp.float32)
    factor = factor.at[pivots].set(lower).at[kept].set(side_factor)
    return (factor, schur, kept)

def reference(child_fronts, child_map, parent_front):
    tiles = parent_front.reshape(PBLK, TILE, PBLK, TILE).transpose(0, 2, 1, 3)
    factors = []
    for child in range(CHILDREN):
        factor, schur, kept = partial_factor(child_fronts[child], CBLK, CBLK // STEPS)
        parts = schur.reshape(KEPT, TILE, KEPT, TILE).transpose(0, 2, 1, 3)
        chosen = child_map[child]
        tiles = tiles.at[chosen[:, None], chosen[None, :]].add(parts)
        factors.append(factor)
    assembled = tiles.transpose(0, 2, 1, 3).reshape(PARENT_ORDER, PARENT_ORDER)
    parent_factor, schur, kept = partial_factor(assembled, PBLK, PBLK // STEPS)
    parent_update = jnp.zeros_like(assembled).at[kept[:, None], kept[None, :]].set(schur)
    return (jnp.stack(factors), parent_factor, parent_update)
```

```python
import functools

import jax
import jax.numpy as jnp
from jax import lax
from jax.experimental import pallas as pl
from jax.experimental.pallas import tpu as pltpu
from jax.sharding import PartitionSpec as P

TILE = 128
STEPS = 8
CBLK = 64
PBLK = 96
ORDER = TILE * STEPS

SWAP = [(0, 1), (1, 0)]
GROUP = ("sub", "y")
COL = ("xlo", "z")
VMEM = pl.BlockSpec(memory_space=pltpu.VMEM)
SMEM = pl.BlockSpec(memory_space=pltpu.SMEM)


def split(x):
    high = x.astype(jnp.bfloat16)
    return high, (x - high.astype(jnp.float32)).astype(jnp.bfloat16)


def dot3(a, b, contract):
    dot = functools.partial(
        lax.dot_general, dimension_numbers=(contract, ((), ())), preferred_element_type=jnp.float32
    )
    return dot(a[0], b[0]) + (dot(a[0], b[1]) + dot(a[1], b[0]))


def factor_tile(s_ref, u_ref, x_ref):
    full = (8, TILE)
    lane = lax.broadcasted_iota(jnp.int32, full, 1)
    sub = lax.broadcasted_iota(jnp.int32, full, 0)
    for p in range(TILE // 8):
        j0 = 8 * p
        inside = (lane >= j0) & (lane < j0 + 8)
        panel = s_ref[j0 : j0 + 8, :]
        cols = [jnp.broadcast_to(panel[:, j0 + k : j0 + k + 1], full) for k in range(8)]
        c = [[jnp.broadcast_to(cols[m][k : k + 1, :], full) if m >= k else None for m in range(8)] for k in range(8)]
        low = [[None] * 8 for _ in range(8)]
        inv, root = [None] * 8, [None] * 8
        for k in range(8):
            root[k] = lax.rsqrt(c[k][k])
            inv[k] = root[k] * root[k]
            for m in range(k + 1, 8):
                low[m][k] = c[k][m] * inv[k]
            for m in range(k + 1, 8):
                for n in range(m, 8):
                    c[m][n] = c[m][n] - low[m][k] * c[k][n]
        e = []
        for k in range(8):
            row = jnp.broadcast_to(panel[k : k + 1, :], full)
            row = jnp.where(inside, jnp.where(lane == j0 + k, 1.0, 0.0), row)
            for m in range(k):
                row = row - low[k][m] * e[m]
            e.append(row)
        q = [None] * 8
        for k in reversed(range(8)):
            row = inv[k] * e[k]
            for m in range(k + 1, 8):
                row = row - low[m][k] * q[m]
            q[k] = row
        out = jnp.zeros(full, jnp.float32)
        diag = jnp.zeros(full, jnp.float32)
        for k in range(8):
            out = jnp.where(sub == k, e[k] * root[k], out)
            for m in range(k, 8):
                diag = jnp.where((sub == k) & (lane == j0 + m), c[k][m] * root[k], diag)
        x_ref[j0 : j0 + 8, :] = jnp.where(lane < j0 + 8, out, 0.0)
        u_ref[j0 : j0 + 8, :] = jnp.where(lane >= j0 + 8, out, diag)
        for i in range(p + 1, TILE // 8):
            old = s_ref[8 * i : 8 * i + 8, :]
            new = jnp.where(inside, 0.0, old)
            for k in range(8):
                new = new - jnp.broadcast_to(old[:, j0 + k : j0 + k + 1], full) * q[k]
            s_ref[8 * i : 8 * i + 8, :] = new


def factor_kernel(core_ref, own_ref, other_ref, u_ref, x_ref, w_ref, s_ref, uk_ref, xk_ref, row_ref):
    core = core_ref[0]
    groups, depth = own_ref.shape[1], own_ref.shape[2]
    pitch = ORDER // groups
    for ref, which in ((own_ref, core), (other_ref, 1 - core)):
        for g in range(groups):
            begin = pl.multiple_of(g * pitch + which * depth, depth)
            for c in range(STEPS):
                w_ref[pl.ds(begin, depth), c * TILE : (c + 1) * TILE] = ref[c, g]
    block = lax.broadcasted_iota(jnp.int32, (TILE, ORDER), 1) // TILE

    def step(k, carry):
        here = pl.ds(pl.multiple_of(k * TILE, TILE), TILE)
        s_ref[...] = w_ref[here, here]
        factor_tile(s_ref, uk_ref, xk_ref)
        row_ref[...] = dot3(split(xk_ref[...]), split(w_ref[here, :]), ((1,), (0,)))
        row_ref[:, here] = xk_ref[...]
        new = row_ref[...]
        x_ref[here, :] = jnp.where(block <= k, new, 0.0)
        u_ref[here, :] = jnp.where(block > k, new, 0.0)
        u_ref[here, here] = uk_ref[...]
        right = split(new)

        def trail(i, carry):
            at = pl.ds(pl.multiple_of(i * TILE, TILE), TILE)
            w_ref[at, here] = jnp.zeros((TILE, TILE), jnp.float32)
            w_ref[at, :] -= dot3(split(row_ref[:, at].T), right, ((1,), (0,)))
            return carry

        lax.fori_loop(k + 1, STEPS, trail, 0)
        return carry

    lax.fori_loop(0, STEPS, step, 0)


def factor(core, own, other):
    out = jax.ShapeDtypeStruct((ORDER, ORDER), jnp.float32)
    return pl.pallas_call(
        factor_kernel,
        out_shape=(out, out),
        in_specs=[SMEM, VMEM, VMEM],
        out_specs=(VMEM, VMEM),
        scratch_shapes=[pltpu.VMEM((ORDER, ORDER), jnp.float32)]
        + [pltpu.VMEM((TILE, TILE), jnp.float32)] * 3
        + [pltpu.VMEM((TILE, ORDER), jnp.float32)],
        compiler_params=pltpu.CompilerParams(vmem_limit_bytes=40 << 20),
        cost_estimate=pl.CostEstimate(flops=100_000_000_000, bytes_accessed=16 << 20, transcendentals=0),
        name="factor",
    )(core.reshape(1), own, other)


def solve_panels(col, cols_ref, x_ref, factor_ref, xs, cs, rs, ls, ts):
    wide = 2 * TILE
    xs[0][...], xs[1][...] = split(x_ref[...])
    for c in range(STEPS):
        at = slice(c * TILE, (c + 1) * TILE)
        cs[0][:, at], cs[1][:, at] = split(cols_ref[c])
    for k in range(STEPS // 2):
        depth = wide * (k + 1)
        at = slice(k * wide, depth)
        x_now = (xs[0][at, :depth], xs[1][at, :depth])
        left = dot3((cs[0][:, :depth], cs[1][:, :depth]), x_now, ((1,), (1,)))
        ls[0][:, at], ls[1][:, at] = split(left)
        for half in range(2):

            @pl.when(col == 2 * k + half)
            def _():
                factor_ref[...] = left[:, half * TILE : (half + 1) * TILE]

        def turn(n, carry):
            here = pl.ds(pl.multiple_of(n * wide, wide), wide)
            right = dot3(x_now, (rs[0][:depth, here], rs[1][:depth, here]), ((1,), (0,)))
            ts[0][at, here], ts[1][at, here] = split(right)
            return carry

        lax.fori_loop(0, rs[0].shape[1] // wide, turn, 0)


def child_kernel(where_ref, front_ref, cols_ref, rows_ref, x_ref, lower_ref, box_ref, factor_ref, *scratch):
    xs, cs, rs, ls, ts = (scratch[i : i + 2] for i in range(0, 10, 2))
    wide = 2 * TILE
    col = where_ref[0]
    rs[0][...], rs[1][...] = split(rows_ref[...])
    solve_panels(col, cols_ref, x_ref, factor_ref, xs, cs, rs, ls, ts)
    factor_ref[:TILE, :] = lower_ref[...]
    left = (ls[0][...], ls[1][...])

    def chunk(n, carry):
        here = pl.ds(pl.multiple_of(n * wide, wide), wide)
        schur = front_ref[:, here] - dot3(left, (ts[0][:, here], ts[1][:, here]), ((1,), (0,)))
        for half in range(2):
            b = 2 * n + half

            @pl.when(b > 0)
            def _():
                for a in range(1, STEPS):
                    slot = where_ref[a] * STEPS + where_ref[STEPS + b]
                    box_ref[slot] = schur[a * TILE : (a + 1) * TILE, half * TILE : (half + 1) * TILE]

        return carry

    lax.fori_loop(0, front_ref.shape[1] // wide, chunk, 0)


def panel_scratch(rows, cols):
    shapes = [(ORDER, ORDER), (rows, ORDER), (ORDER, cols), (rows, ORDER), (ORDER, cols)]
    return [pltpu.VMEM(shape, jnp.bfloat16) for shape in shapes for _ in range(2)]


def child_update(where, front, cols, rows, x, lower):
    return pl.pallas_call(
        child_kernel,
        out_shape=(
            jax.ShapeDtypeStruct((STEPS * STEPS, TILE, TILE), jnp.float32),
            jax.ShapeDtypeStruct((front.shape[0], TILE), jnp.float32),
        ),
        in_specs=[SMEM] + [VMEM] * 5,
        out_specs=(VMEM, VMEM),
        scratch_shapes=panel_scratch(*front.shape),
        compiler_params=pltpu.CompilerParams(vmem_limit_bytes=58 << 20),
        name="child_update",
    )(where, front, cols, rows, x, lower)


def parent_kernel(where_ref, front_ref, cols_ref, own_ref, other_ref, x_ref, lower_ref, out_ref, factor_ref, *scratch):
    xs, cs, rs, ls, ts = (scratch[i : i + 2] for i in range(0, 10, 2))
    wide = 2 * TILE
    col, core = where_ref[0], where_ref[1]
    depth = own_ref.shape[1]
    for ref, which in ((own_ref, core), (other_ref, 1 - core)):
        for g in range(STEPS):
            at = pl.ds(pl.multiple_of(g * TILE + which * depth, depth), depth)
            rs[0][at, :], rs[1][at, :] = split(ref[g])
    solve_panels(col, cols_ref, x_ref, factor_ref, xs, cs, rs, ls, ts)

    @pl.when(core == 0)
    def _():
        factor_ref[:TILE, :] = lower_ref[...]

    left = (ls[0][...], ls[1][...])

    def chunk(n, carry):
        here = pl.ds(pl.multiple_of(n * wide, wide), wide)
        out_ref[:, here] = front_ref[:, here] - dot3(left, (ts[0][:, here], ts[1][:, here]), ((1,), (0,)))
        return carry

    lax.fori_loop(0, front_ref.shape[1] // wide, chunk, 0)
    out_ref[:, :TILE] = jnp.zeros((front_ref.shape[0], TILE), jnp.float32)

    @pl.when(core == 0)
    def _():
        out_ref[:TILE, :] = jnp.zeros((TILE, front_ref.shape[1]), jnp.float32)


def parent_update(where, front, cols, own, other, x, lower):
    return pl.pallas_call(
        parent_kernel,
        out_shape=(
            jax.ShapeDtypeStruct(front.shape, jnp.float32),
            jax.ShapeDtypeStruct((front.shape[0], TILE), jnp.float32),
        ),
        in_specs=[SMEM] + [VMEM] * 6,
        out_specs=(VMEM, VMEM),
        scratch_shapes=panel_scratch(*front.shape),
        compiler_params=pltpu.CompilerParams(vmem_limit_bytes=60 << 20),
        name="parent_update",
    )(where, front, cols, own, other, x, lower)


def assemble_kernel(rows_ref, cols_ref, front_ref, own_ref, other_ref, out_ref):
    tiles_row, tiles_col = (n // TILE for n in front_ref.shape)
    out_ref[...] = front_ref[...]
    for child in range(2):
        for i in range(tiles_row):
            source = rows_ref[child * tiles_row + i]

            def add(box_ref, base):
                at = slice(i * TILE, (i + 1) * TILE)
                for j in range(tiles_col):
                    place = cols_ref[child * tiles_col + j]

                    @pl.when(place >= 0)
                    def _():
                        out_ref[at, j * TILE : (j + 1) * TILE] += box_ref[base + place]

            @pl.when((source >= 0) & (source < STEPS * STEPS))
            def _():
                add(own_ref, source)

            @pl.when(source >= STEPS * STEPS)
            def _():
                add(other_ref, source - STEPS * STEPS)


def assemble(rows, cols, front, own, other):
    return pl.pallas_call(
        assemble_kernel,
        out_shape=jax.ShapeDtypeStruct(front.shape, jnp.float32),
        in_specs=[SMEM, SMEM] + [VMEM] * 3,
        out_specs=VMEM,
        compiler_params=pltpu.CompilerParams(vmem_limit_bytes=40 << 20),
        name="assemble",
    )(rows, cols, front, own, other)


def spread(x, axes):
    count = lax.axis_size(axes)
    copies = jnp.broadcast_to(x[None], (count,) + x.shape)
    return lax.all_to_all(copies, axes, 0, 0, tiled=True)


def after(x, first):
    return lax.optimization_barrier((x, first))[0]


def local(child_fronts, child_map, parent_front):
    child = lax.axis_index("sub")
    core = lax.axis_index("core")
    row = lax.axis_index(("y", "core"))
    col = lax.axis_index(COL)
    group = lax.axis_index(GROUP)
    front = child_fronts[0]
    kept = CBLK // STEPS - 1

    own = spread(spread(front[:TILE, :TILE], "y"), COL)
    other = lax.ppermute(own, "core", SWAP)
    columns = lax.all_gather(after(front[:, :TILE], other), COL, axis=0)
    rows = lax.all_gather(after(front[:TILE, :], other), ("y", "core"), axis=0, tiled=True)
    upper, inverse = factor(core, own, other)
    lower = lax.dynamic_slice(upper, (col * TILE, row * TILE), (TILE, TILE)).T
    mine = child_map[child] // (PBLK // STEPS)
    zero = jnp.zeros((1,), jnp.int32)
    where = jnp.concatenate(
        [
            col.reshape(1),
            lax.dynamic_slice(mine, (row * kept,), (kept,)),
            zero,
            lax.dynamic_slice(mine, (col * kept,), (kept,)),
        ]
    ).astype(jnp.int32)
    box, child_factor = child_update(where, front, columns, rows, inverse, lower)

    box = lax.all_to_all(box, GROUP + COL, 0, 0, tiled=True)
    box_other = lax.ppermute(box, "core", SWAP)
    tiles_row, tiles_col = parent_front.shape[0] // TILE, parent_front.shape[1] // TILE
    blocks = jnp.arange(PBLK, dtype=jnp.int32)
    number = jnp.arange(CBLK - STEPS, dtype=jnp.int32)
    source = jnp.max(jnp.where(child_map[:, :, None] == blocks, number[:, None], -1), axis=1)
    source_row = lax.dynamic_slice(source, (0, (2 * group + core) * tiles_row), (2, tiles_row))
    source_col = lax.dynamic_slice(source, (0, col * tiles_col), (2, tiles_col))
    whose = (source_row // kept % 2 != core).astype(jnp.int32) * (STEPS * STEPS)
    place = whose + jnp.arange(2, dtype=jnp.int32)[:, None] * (STEPS * STEPS // 2) + source_row // (2 * kept) * STEPS
    place_row = jnp.where(source_row >= 0, place, -1)
    place_col = jnp.where(source_col >= 0, source_col // kept, -1)
    front = assemble(place_row.reshape(-1), place_col.reshape(-1), parent_front, box, box_other)

    down = [(0, 1)]
    half = TILE // 2
    piece = jnp.where(core == 0, front[:half, :TILE], lax.ppermute(front[half:TILE, :TILE], "core", down))
    own = spread(spread(piece, GROUP), COL)
    other = lax.ppermute(own, "core", SWAP)
    columns = lax.all_gather(after(front[:, :TILE], other), COL, axis=0)
    strip = jnp.where(core == 0, front[:half, :], lax.ppermute(front[half:TILE, :], "core", down))
    rows_own = spread(after(strip, other), GROUP)
    rows_other = lax.ppermute(rows_own, "core", SWAP)
    upper, inverse = factor(core, own, other)
    lower = lax.dynamic_slice(upper, (col * TILE, group * TILE), (TILE, TILE)).T
    where = jnp.stack([col, core]).astype(jnp.int32)
    update, parent_factor = parent_update(where, front, columns, rows_own, rows_other, inverse, lower)
    return (child_factor[None], parent_factor, update)


def solution(mesh):
    shape = (2, 4, 2, 2, 4)
    fine = jax.sharding.Mesh(mesh.devices.reshape(shape), ("sub", "y", "core", "xlo", "z"))
    in_specs = (P("sub", ("y", "core"), COL), P(), P(("sub", "y", "core"), COL))
    out_specs = (P("sub", ("y", "core"), COL), P(("sub", "y", "core"), COL), P(("sub", "y", "core"), COL))
    return jax.shard_map(local, mesh=fine, in_specs=in_specs, out_specs=out_specs, check_vma=False)
```

```python
import functools

import jax
import jax.numpy as jnp
from jax import lax
from jax.experimental import pallas as pl
from jax.experimental.pallas import tpu as pltpu
from jax.sharding import PartitionSpec as P

TILE = 128
STEPS = 8
CBLK = 64
PBLK = 96
ORDER = TILE * STEPS

SWAP = [(0, 1), (1, 0)]
GROUP = ("sub", "y")
COL = ("xlo", "z")
VMEM = pl.BlockSpec(memory_space=pltpu.VMEM)
SMEM = pl.BlockSpec(memory_space=pltpu.SMEM)


def split(x):
    high = x.astype(jnp.bfloat16)
    return high, (x - high.astype(jnp.float32)).astype(jnp.bfloat16)


def dot3(a, b, contract):
    dot = functools.partial(
        lax.dot_general, dimension_numbers=(contract, ((), ())), preferred_element_type=jnp.float32
    )
    return dot(a[0], b[0]) + (dot(a[0], b[1]) + dot(a[1], b[0]))


def factor_tile(s_ref, u_ref, x_ref, beside):
    full = (8, TILE)
    count = TILE // 8
    lane = lax.broadcasted_iota(jnp.int32, full, 1)
    sub = lax.broadcasted_iota(jnp.int32, full, 0)
    s = [s_ref[8 * i : 8 * i + 8, :] for i in range(count)]
    for p in range(count):
        j0 = 8 * p
        inside = (lane >= j0) & (lane < j0 + 8)
        panel = s[p]
        if p == 0:
            cols = [jnp.broadcast_to(panel[:, j0 + k : j0 + k + 1], full) for k in range(8)]
        c = [[jnp.broadcast_to(cols[m][k : k + 1, :], full) if m >= k else None for m in range(8)] for k in range(8)]
        e = []
        for k in range(8):
            row = jnp.broadcast_to(panel[k : k + 1, :], full)
            e.append(jnp.where(inside, jnp.where(lane == j0 + k, 1.0, 0.0), row))
        more = p + 1 < count
        if more:
            f = [jnp.broadcast_to(s[p + 1][:, j0 + k : j0 + k + 1], full) for k in range(8)]
            later = jnp.where(inside, 0.0, s[p + 1])
            cols = [jnp.broadcast_to(s[p + 1][:, j0 + 8 + k : j0 + 9 + k], full) for k in range(8)]
        root = [None] * 8
        for k in range(8):
            root[k] = lax.rsqrt(c[k][k])
            for m in range(k, 8):
                c[k][m] = c[k][m] * root[k]
            e[k] = e[k] * root[k]
            if more:
                f[k] = f[k] * root[k]
                later = later - f[k] * e[k]
                for n in range(8):
                    cols[n] = cols[n] - f[k] * jnp.broadcast_to(f[k][n : n + 1, :], full)
            for m in range(k + 1, 8):
                for n in range(m, 8):
                    c[m][n] = c[m][n] - c[k][m] * c[k][n]
                e[m] = e[m] - c[k][m] * e[k]
                if more:
                    f[m] = f[m] - c[k][m] * f[k]
        beside(p)
        if p + 2 < count:
            q = [None] * 8
            for k in reversed(range(8)):
                row = e[k]
                for m in range(k + 1, 8):
                    row = row - c[k][m] * q[m]
                q[k] = row * root[k]
            for i in range(p + 2, count):
                new = jnp.where(inside, 0.0, s[i])
                for k in range(8):
                    new = new - jnp.broadcast_to(s[i][:, j0 + k : j0 + k + 1], full) * q[k]
                s[i] = new
        if more:
            s[p + 1] = later
        out = jnp.zeros(full, jnp.float32)
        diag = jnp.zeros(full, jnp.float32)
        for k in range(8):
            out = jnp.where(sub == k, e[k], out)
            for m in range(k, 8):
                diag = jnp.where((sub == k) & (lane == j0 + m), c[k][m], diag)
        x_ref[j0 : j0 + 8, :] = jnp.where(lane < j0 + 8, out, 0.0)
        u_ref[j0 : j0 + 8, :] = jnp.where(lane >= j0 + 8, out, diag)


def factor_kernel(where_ref, own_ref, other_ref, x_ref, lower_ref, w_ref, u_ref, d_ref, s_ref, xn_ref, xk_ref, last_ref, high_ref, rest_ref):
    core, tile_row, tile_col = where_ref[0], where_ref[1], where_ref[2]
    groups, depth = own_ref.shape[1], own_ref.shape[2]
    pitch = ORDER // groups
    for ref, which in ((own_ref, core), (other_ref, 1 - core)):
        for g in range(groups):
            begin = pl.multiple_of(g * pitch + which * depth, depth)
            for c in range(STEPS):
                w_ref[pl.ds(begin, depth), c * TILE : (c + 1) * TILE] = ref[c, g]
    block = lax.broadcasted_iota(jnp.int32, (TILE, ORDER), 1) // TILE

    def place(k):
        return pl.ds(pl.multiple_of(k * TILE, TILE), TILE)

    def finish(k):
        row = dot3(split(xk_ref[...]), split(w_ref[place(k), :]), ((1,), (0,)))
        last_ref[...] = row
        last_ref[:, place(k)] = xk_ref[...]
        row = last_ref[...]
        x_ref[place(k), :] = jnp.where(block <= k, row, 0.0)
        u_ref[place(k), :] = jnp.where(block > k, row, 0.0)
        high_ref[...], rest_ref[...] = split(row)

    def step(k, carry):
        before = k - 1

        def beside(p):
            if p == 0:
                finish(jnp.maximum(before, 0))
            elif p % 2 == 0:
                i = p // 2
                at = slice(i * TILE, (i + 1) * TILE)
                mine = jnp.where(i > before, last_ref[:, at], 0.0).T
                held = w_ref[at, :]
                held = jnp.where((block == before) & (i > before), 0.0, held)
                w_ref[at, :] = held - dot3(split(mine), (high_ref[...], rest_ref[...]), ((1,), (0,)))

        factor_tile(s_ref, d_ref.at[place(k)], xn_ref, beside)
        xk_ref[...] = xn_ref[...]
        after_k = jnp.minimum(k + 1, STEPS - 1)
        high, rest = split(dot3(split(xn_ref[...]), split(w_ref[place(k), place(after_k)]), ((1,), (0,))))
        s_ref[...] = w_ref[place(after_k), place(after_k)] - dot3((high.T, rest.T), (high, rest), ((1,), (0,)))
        return carry

    xk_ref[...] = jnp.zeros((TILE, TILE), jnp.float32)
    s_ref[...] = w_ref[:TILE, :TILE]
    lax.fori_loop(0, STEPS, step, 0)
    finish(STEPS - 1)
    tile = jnp.where(tile_row == tile_col, d_ref[place(tile_col), :], u_ref[place(tile_col), place(tile_row)])
    lower_ref[...] = tile.T


def factor(where, own, other):
    return pl.pallas_call(
        factor_kernel,
        out_shape=(
            jax.ShapeDtypeStruct((ORDER, ORDER), jnp.float32),
            jax.ShapeDtypeStruct((TILE, TILE), jnp.float32),
        ),
        in_specs=[SMEM, VMEM, VMEM],
        out_specs=(VMEM, VMEM),
        scratch_shapes=[pltpu.VMEM((ORDER, ORDER), jnp.float32)] * 2
        + [pltpu.VMEM((ORDER, TILE), jnp.float32)]
        + [pltpu.VMEM((TILE, TILE), jnp.float32)] * 3
        + [pltpu.VMEM((TILE, ORDER), jnp.float32)]
        + [pltpu.VMEM((TILE, ORDER), jnp.bfloat16)] * 2,
        compiler_params=pltpu.CompilerParams(vmem_limit_bytes=40 << 20),
        cost_estimate=pl.CostEstimate(flops=100_000_000_000, bytes_accessed=16 << 20, transcendentals=0),
        name="factor",
    )(where, own, other)


def solve_panels(col, cols_ref, x_ref, factor_ref, xs, cs, rs, ls, ts):
    wide = 2 * TILE
    xs[0][...], xs[1][...] = split(x_ref[...])
    for c in range(STEPS):
        at = slice(c * TILE, (c + 1) * TILE)
        cs[0][:, at], cs[1][:, at] = split(cols_ref[c])
    for k in range(STEPS // 2):
        depth = wide * (k + 1)
        at = slice(k * wide, depth)
        x_now = (xs[0][at, :depth], xs[1][at, :depth])
        left = dot3((cs[0][:, :depth], cs[1][:, :depth]), x_now, ((1,), (1,)))
        ls[0][:, at], ls[1][:, at] = split(left)
        for half in range(2):

            @pl.when(col == 2 * k + half)
            def _():
                factor_ref[...] = left[:, half * TILE : (half + 1) * TILE]

        def turn(n, carry):
            here = pl.ds(pl.multiple_of(n * wide, wide), wide)
            right = dot3(x_now, (rs[0][:depth, here], rs[1][:depth, here]), ((1,), (0,)))
            ts[0][at, here], ts[1][at, here] = split(right)
            return carry

        lax.fori_loop(0, rs[0].shape[1] // wide, turn, 0)


def child_kernel(where_ref, front_ref, cols_ref, rows_ref, x_ref, lower_ref, box_ref, factor_ref, *scratch):
    xs, cs, rs, ls, ts = (scratch[i : i + 2] for i in range(0, 10, 2))
    wide = 2 * TILE
    col = where_ref[0]
    rs[0][...], rs[1][...] = split(rows_ref[...])
    solve_panels(col, cols_ref, x_ref, factor_ref, xs, cs, rs, ls, ts)
    factor_ref[:TILE, :] = lower_ref[...]
    left = (ls[0][...], ls[1][...])

    def chunk(n, carry):
        here = pl.ds(pl.multiple_of(n * wide, wide), wide)
        schur = front_ref[:, here] - dot3(left, (ts[0][:, here], ts[1][:, here]), ((1,), (0,)))
        for half in range(2):
            b = 2 * n + half

            @pl.when(b > 0)
            def _():
                for a in range(1, STEPS):
                    slot = where_ref[a] * STEPS + where_ref[STEPS + b]
                    box_ref[slot] = schur[a * TILE : (a + 1) * TILE, half * TILE : (half + 1) * TILE]

        return carry

    lax.fori_loop(0, front_ref.shape[1] // wide, chunk, 0)


def panel_scratch(rows, cols):
    shapes = [(ORDER, ORDER), (rows, ORDER), (ORDER, cols), (rows, ORDER), (ORDER, cols)]
    return [pltpu.VMEM(shape, jnp.bfloat16) for shape in shapes for _ in range(2)]


def child_update(where, front, cols, rows, x, lower):
    return pl.pallas_call(
        child_kernel,
        out_shape=(
            jax.ShapeDtypeStruct((STEPS * STEPS, TILE, TILE), jnp.float32),
            jax.ShapeDtypeStruct((front.shape[0], TILE), jnp.float32),
        ),
        in_specs=[SMEM] + [VMEM] * 5,
        out_specs=(VMEM, VMEM),
        scratch_shapes=panel_scratch(*front.shape),
        compiler_params=pltpu.CompilerParams(vmem_limit_bytes=58 << 20),
        name="child_update",
    )(where, front, cols, rows, x, lower)


def parent_kernel(where_ref, front_ref, cols_ref, own_ref, other_ref, x_ref, lower_ref, out_ref, factor_ref, *scratch):
    xs, cs, rs, ls, ts = (scratch[i : i + 2] for i in range(0, 10, 2))
    wide = 2 * TILE
    col, core = where_ref[0], where_ref[1]
    depth = own_ref.shape[1]
    for ref, which in ((own_ref, core), (other_ref, 1 - core)):
        for g in range(STEPS):
            at = pl.ds(pl.multiple_of(g * TILE + which * depth, depth), depth)
            rs[0][at, :], rs[1][at, :] = split(ref[g])
    solve_panels(col, cols_ref, x_ref, factor_ref, xs, cs, rs, ls, ts)

    @pl.when(core == 0)
    def _():
        factor_ref[:TILE, :] = lower_ref[...]

    left = (ls[0][...], ls[1][...])

    def chunk(n, carry):
        here = pl.ds(pl.multiple_of(n * wide, wide), wide)
        out_ref[:, here] = front_ref[:, here] - dot3(left, (ts[0][:, here], ts[1][:, here]), ((1,), (0,)))
        return carry

    lax.fori_loop(0, front_ref.shape[1] // wide, chunk, 0)
    out_ref[:, :TILE] = jnp.zeros((front_ref.shape[0], TILE), jnp.float32)

    @pl.when(core == 0)
    def _():
        out_ref[:TILE, :] = jnp.zeros((TILE, front_ref.shape[1]), jnp.float32)


def parent_update(where, front, cols, own, other, x, lower):
    return pl.pallas_call(
        parent_kernel,
        out_shape=(
            jax.ShapeDtypeStruct(front.shape, jnp.float32),
            jax.ShapeDtypeStruct((front.shape[0], TILE), jnp.float32),
        ),
        in_specs=[SMEM] + [VMEM] * 6,
        out_specs=(VMEM, VMEM),
        scratch_shapes=panel_scratch(*front.shape),
        compiler_params=pltpu.CompilerParams(vmem_limit_bytes=60 << 20),
        name="parent_update",
    )(where, front, cols, own, other, x, lower)


def assemble_kernel(rows_ref, cols_ref, front_ref, own_ref, other_ref, out_ref):
    tiles_row, tiles_col = (n // TILE for n in front_ref.shape)
    out_ref[...] = front_ref[...]
    for child in range(2):
        for i in range(tiles_row):
            source = rows_ref[child * tiles_row + i]

            def add(box_ref, base):
                at = slice(i * TILE, (i + 1) * TILE)
                for j in range(tiles_col):
                    place = cols_ref[child * tiles_col + j]

                    @pl.when(place >= 0)
                    def _():
                        out_ref[at, j * TILE : (j + 1) * TILE] += box_ref[base + place]

            @pl.when((source >= 0) & (source < STEPS * STEPS))
            def _():
                add(own_ref, source)

            @pl.when(source >= STEPS * STEPS)
            def _():
                add(other_ref, source - STEPS * STEPS)


def assemble(rows, cols, front, own, other):
    return pl.pallas_call(
        assemble_kernel,
        out_shape=jax.ShapeDtypeStruct(front.shape, jnp.float32),
        in_specs=[SMEM, SMEM] + [VMEM] * 3,
        out_specs=VMEM,
        compiler_params=pltpu.CompilerParams(vmem_limit_bytes=40 << 20),
        name="assemble",
    )(rows, cols, front, own, other)


def spread(x, axes):
    count = lax.axis_size(axes)
    copies = jnp.broadcast_to(x[None], (count,) + x.shape)
    return lax.all_to_all(copies, axes, 0, 0, tiled=True)


def after(x, first):
    return lax.optimization_barrier((x, first))[0]


def local(child_fronts, child_map, parent_front):
    child = lax.axis_index("sub")
    core = lax.axis_index("core")
    row = lax.axis_index(("y", "core"))
    col = lax.axis_index(COL)
    group = lax.axis_index(GROUP)
    front = child_fronts[0]
    kept = CBLK // STEPS - 1

    first = spread(front[:TILE, :TILE], "y")
    rows = lax.all_gather(after(front[:TILE, :], first), ("y", "core"), axis=0, tiled=True)
    own = spread(first, COL)
    other = lax.ppermute(own, "core", SWAP)
    columns = lax.all_gather(after(front[:, :TILE], own), COL, axis=0)
    inverse, lower = factor(jnp.stack([core, row, col]).astype(jnp.int32), own, other)
    mine = child_map[child] // (PBLK // STEPS)
    zero = jnp.zeros((1,), jnp.int32)
    where = jnp.concatenate(
        [
            col.reshape(1),
            lax.dynamic_slice(mine, (row * kept,), (kept,)),
            zero,
            lax.dynamic_slice(mine, (col * kept,), (kept,)),
        ]
    ).astype(jnp.int32)
    box, child_factor = child_update(where, front, columns, rows, inverse, lower)

    box = lax.all_to_all(box, GROUP + COL, 0, 0, tiled=True)
    box_other = lax.ppermute(box, "core", SWAP)
    tiles_row, tiles_col = parent_front.shape[0] // TILE, parent_front.shape[1] // TILE
    blocks = jnp.arange(PBLK, dtype=jnp.int32)
    number = jnp.arange(CBLK - STEPS, dtype=jnp.int32)
    source = jnp.max(jnp.where(child_map[:, :, None] == blocks, number[:, None], -1), axis=1)
    source_row = lax.dynamic_slice(source, (0, (2 * group + core) * tiles_row), (2, tiles_row))
    source_col = lax.dynamic_slice(source, (0, col * tiles_col), (2, tiles_col))
    whose = (source_row // kept % 2 != core).astype(jnp.int32) * (STEPS * STEPS)
    place = whose + jnp.arange(2, dtype=jnp.int32)[:, None] * (STEPS * STEPS // 2) + source_row // (2 * kept) * STEPS
    place_row = jnp.where(source_row >= 0, place, -1)
    place_col = jnp.where(source_col >= 0, source_col // kept, -1)
    front = assemble(place_row.reshape(-1), place_col.reshape(-1), parent_front, box, box_other)

    down = [(0, 1)]
    half = TILE // 2
    piece = jnp.where(core == 0, front[:half, :TILE], lax.ppermute(front[half:TILE, :TILE], "core", down))
    first = spread(piece, GROUP)
    strip = jnp.where(core == 0, front[:half, :], lax.ppermute(front[half:TILE, :], "core", down))
    rows_own = spread(after(strip, first), GROUP)
    own = spread(first, COL)
    other = lax.ppermute(own, "core", SWAP)
    columns = lax.all_gather(after(front[:, :TILE], own), COL, axis=0)
    inverse, lower = factor(jnp.stack([core, group, col]).astype(jnp.int32), own, other)
    rows_own = after(rows_own, lower)
    rows_other = lax.ppermute(rows_own, "core", SWAP)
    where = jnp.stack([col, core]).astype(jnp.int32)
    update, parent_factor = parent_update(where, front, columns, rows_own, rows_other, inverse, lower)
    return (child_factor[None], parent_factor, update)


def solution(mesh):
    shape = (2, 4, 2, 2, 4)
    fine = jax.sharding.Mesh(mesh.devices.reshape(shape), ("sub", "y", "core", "xlo", "z"))
    in_specs = (P("sub", ("y", "core"), COL), P(), P(("sub", "y", "core"), COL))
    out_specs = (P("sub", ("y", "core"), COL), P(("sub", "y", "core"), COL), P(("sub", "y", "core"), COL))
    return jax.shard_map(local, mesh=fine, in_specs=in_specs, out_specs=out_specs, check_vma=False)
```

```python
import functools

import jax
import jax.numpy as jnp
from jax import lax
from jax.experimental import pallas as pl
from jax.experimental.pallas import tpu as pltpu
from jax.sharding import PartitionSpec as P

TILE = 128
STEPS = 8
CBLK = 64
PBLK = 96
ORDER = TILE * STEPS

SWAP = [(0, 1), (1, 0)]
GROUP = ("sub", "y")
COL = ("xlo", "z")
VMEM = pl.BlockSpec(memory_space=pltpu.VMEM)
SMEM = pl.BlockSpec(memory_space=pltpu.SMEM)
ANY = pl.BlockSpec(memory_space=pl.ANY)


def split(x):
    high = x.astype(jnp.bfloat16)
    return high, (x - high.astype(jnp.float32)).astype(jnp.bfloat16)


def dot3(a, b, contract):
    dot = functools.partial(
        lax.dot_general, dimension_numbers=(contract, ((), ())), preferred_element_type=jnp.float32
    )
    return dot(a[0], b[0]) + (dot(a[0], b[1]) + dot(a[1], b[0]))


def factor_tile(s_ref, u_ref, x_ref, beside):
    full = (8, TILE)
    count = TILE // 8
    lane = lax.broadcasted_iota(jnp.int32, full, 1)
    sub = lax.broadcasted_iota(jnp.int32, full, 0)
    s = [s_ref[8 * i : 8 * i + 8, :] for i in range(count)]
    for p in range(count):
        j0 = 8 * p
        inside = (lane >= j0) & (lane < j0 + 8)
        panel = s[p]
        if p == 0:
            cols = [jnp.broadcast_to(panel[:, j0 + k : j0 + k + 1], full) for k in range(8)]
        c = [[jnp.broadcast_to(cols[m][k : k + 1, :], full) if m >= k else None for m in range(8)] for k in range(8)]
        e = []
        for k in range(8):
            row = jnp.broadcast_to(panel[k : k + 1, :], full)
            e.append(jnp.where(inside, jnp.where(lane == j0 + k, 1.0, 0.0), row))
        more = p + 1 < count
        if more:
            f = [jnp.broadcast_to(s[p + 1][:, j0 + k : j0 + k + 1], full) for k in range(8)]
            later = jnp.where(inside, 0.0, s[p + 1])
            cols = [jnp.broadcast_to(s[p + 1][:, j0 + 8 + k : j0 + 9 + k], full) for k in range(8)]
        root = [None] * 8
        for k in range(8):
            root[k] = lax.rsqrt(c[k][k])
            for m in range(k, 8):
                c[k][m] = c[k][m] * root[k]
            e[k] = e[k] * root[k]
            if more:
                f[k] = f[k] * root[k]
                later = later - f[k] * e[k]
                for n in range(8):
                    cols[n] = cols[n] - f[k] * jnp.broadcast_to(f[k][n : n + 1, :], full)
            for m in range(k + 1, 8):
                for n in range(m, 8):
                    c[m][n] = c[m][n] - c[k][m] * c[k][n]
                e[m] = e[m] - c[k][m] * e[k]
                if more:
                    f[m] = f[m] - c[k][m] * f[k]
        beside(p)
        if p + 2 < count:
            q = [None] * 8
            for k in reversed(range(8)):
                row = e[k]
                for m in range(k + 1, 8):
                    row = row - c[k][m] * q[m]
                q[k] = row * root[k]
            for i in range(p + 2, count):
                new = jnp.where(inside, 0.0, s[i])
                for k in range(8):
                    new = new - jnp.broadcast_to(s[i][:, j0 + k : j0 + k + 1], full) * q[k]
                s[i] = new
        if more:
            s[p + 1] = later
        out = jnp.zeros(full, jnp.float32)
        diag = jnp.zeros(full, jnp.float32)
        for k in range(8):
            out = jnp.where(sub == k, e[k], out)
            for m in range(k, 8):
                diag = jnp.where((sub == k) & (lane == j0 + m), c[k][m], diag)
        x_ref[j0 : j0 + 8, :] = jnp.where(lane < j0 + 8, out, 0.0)
        u_ref[j0 : j0 + 8, :] = jnp.where(lane >= j0 + 8, out, diag)


def factor_kernel(where_ref, own_ref, other_ref, x_ref, lower_ref, w_ref, u_ref, d_ref, s_ref, xn_ref, xk_ref, last_ref, high_ref, rest_ref):
    core, tile_row, tile_col = where_ref[0], where_ref[1], where_ref[2]
    groups, depth = own_ref.shape[1], own_ref.shape[2]
    pitch = ORDER // groups
    for ref, which in ((own_ref, core), (other_ref, 1 - core)):
        for g in range(groups):
            begin = pl.multiple_of(g * pitch + which * depth, depth)
            for c in range(STEPS):
                w_ref[pl.ds(begin, depth), c * TILE : (c + 1) * TILE] = ref[c, g]
    block = lax.broadcasted_iota(jnp.int32, (TILE, ORDER), 1) // TILE

    def place(k):
        return pl.ds(pl.multiple_of(k * TILE, TILE), TILE)

    def finish(k):
        row = dot3(split(xk_ref[...]), split(w_ref[place(k), :]), ((1,), (0,)))
        last_ref[...] = row
        last_ref[:, place(k)] = xk_ref[...]
        row = last_ref[...]
        x_ref[place(k), :] = jnp.where(block <= k, row, 0.0)
        u_ref[place(k), :] = jnp.where(block > k, row, 0.0)
        high_ref[...], rest_ref[...] = split(row)

    def step(k, carry):
        before = k - 1

        def beside(p):
            if p == 0:
                finish(jnp.maximum(before, 0))
            elif p % 2 == 0:
                i = p // 2
                at = slice(i * TILE, (i + 1) * TILE)
                mine = jnp.where(i > before, last_ref[:, at], 0.0).T
                held = w_ref[at, :]
                held = jnp.where((block == before) & (i > before), 0.0, held)
                w_ref[at, :] = held - dot3(split(mine), (high_ref[...], rest_ref[...]), ((1,), (0,)))

        factor_tile(s_ref, d_ref.at[place(k)], xn_ref, beside)
        xk_ref[...] = xn_ref[...]
        after_k = jnp.minimum(k + 1, STEPS - 1)
        high, rest = split(dot3(split(xn_ref[...]), split(w_ref[place(k), place(after_k)]), ((1,), (0,))))
        s_ref[...] = w_ref[place(after_k), place(after_k)] - dot3((high.T, rest.T), (high, rest), ((1,), (0,)))
        return carry

    xk_ref[...] = jnp.zeros((TILE, TILE), jnp.float32)
    s_ref[...] = w_ref[:TILE, :TILE]
    lax.fori_loop(0, STEPS, step, 0)
    finish(STEPS - 1)
    tile = jnp.where(tile_row == tile_col, d_ref[place(tile_col), :], u_ref[place(tile_col), place(tile_row)])
    lower_ref[...] = tile.T


def factor(where, own, other):
    return pl.pallas_call(
        factor_kernel,
        out_shape=(
            jax.ShapeDtypeStruct((ORDER, ORDER), jnp.float32),
            jax.ShapeDtypeStruct((TILE, TILE), jnp.float32),
        ),
        in_specs=[SMEM, VMEM, VMEM],
        out_specs=(VMEM, VMEM),
        scratch_shapes=[pltpu.VMEM((ORDER, ORDER), jnp.float32)] * 2
        + [pltpu.VMEM((ORDER, TILE), jnp.float32)]
        + [pltpu.VMEM((TILE, TILE), jnp.float32)] * 3
        + [pltpu.VMEM((TILE, ORDER), jnp.float32)]
        + [pltpu.VMEM((TILE, ORDER), jnp.bfloat16)] * 2,
        compiler_params=pltpu.CompilerParams(vmem_limit_bytes=40 << 20),
        cost_estimate=pl.CostEstimate(flops=20_000_000_000, bytes_accessed=16 << 20, transcendentals=0),
        name="factor",
    )(where, own, other)


def chunks(width):
    wide = 2 * TILE
    return [(begin, min(wide, width - begin)) for begin in range(0, width, wide)]


def fetch(pairs, sems):
    copies = [pltpu.make_async_copy(source, target, sems.at[i]) for i, (source, target) in enumerate(pairs)]
    for copy in copies:
        copy.start()
    return copies


def solve_panels(col, copies, x_in, cols_in, rows_in, factor_ref, top, xs, cs, rs, ls, ts):
    wide = 2 * TILE
    copies[0].wait()
    xs[0][...], xs[1][...] = split(x_in[...])
    copies[1].wait()
    for c in range(STEPS):
        at = slice(c * TILE, (c + 1) * TILE)
        cs[0][:, at], cs[1][:, at] = split(cols_in[c])
    for k in range(STEPS // 2):
        depth = wide * (k + 1)
        at = slice(k * wide, depth)
        x_now = (xs[0][at, :depth], xs[1][at, :depth])
        left = dot3((cs[0][:, :depth], cs[1][:, :depth]), x_now, ((1,), (1,)))
        ls[0][:, at], ls[1][:, at] = split(left)
        for half in range(2):

            @pl.when(col == 2 * k + half)
            def _():
                factor_ref[top:, :] = left[:, half * TILE : (half + 1) * TILE]

    copies[2].wait()
    rs[0][...], rs[1][...] = split(rows_in[...])
    for k in range(STEPS // 2):
        depth = wide * (k + 1)
        at = slice(k * wide, depth)
        x_now = (xs[0][at, :depth], xs[1][at, :depth])
        for begin, width in chunks(rows_in.shape[1]):
            here = slice(begin, begin + width)
            right = dot3(x_now, (rs[0][:depth, here], rs[1][:depth, here]), ((1,), (0,)))
            ts[0][at, here], ts[1][at, here] = split(right)


def child_kernel(where_ref, front_ref, cols_ref, rows_ref, x_ref, lower_ref, box_ref, factor_ref, *scratch):
    x_in, cols_in, rows_in, front_in, sems = scratch[:5]
    xs, cs, rs, ls, ts = (scratch[i : i + 2] for i in range(5, 15, 2))
    copies = fetch(
        [(x_ref, x_in), (cols_ref, cols_in), (rows_ref, rows_in), (front_ref.at[TILE:, TILE:], front_in)], sems
    )
    solve_panels(where_ref[0], copies, x_in, cols_in, rows_in, factor_ref, TILE, xs, cs, rs, ls, ts)
    factor_ref[:TILE, :] = lower_ref[...]
    copies[3].wait()
    for begin, width in chunks(front_in.shape[1]):
        here = slice(begin, begin + width)
        left = (ls[0][...], ls[1][...])
        schur = front_in[:, here] - dot3(left, (ts[0][:, here], ts[1][:, here]), ((1,), (0,)))
        for b in range(begin // TILE, (begin + width) // TILE):
            at = slice(b * TILE - begin, (b + 1) * TILE - begin)
            for a in range(STEPS - 1):
                slot = where_ref[1 + a] * STEPS + where_ref[STEPS + b]
                box_ref[slot] = schur[a * TILE : (a + 1) * TILE, at]


def panel_scratch(rows, cols):
    given = [(ORDER, ORDER), (STEPS, rows, TILE), (ORDER, cols), (rows, cols)]
    pairs = [(ORDER, ORDER), (rows, ORDER), (ORDER, cols), (rows, ORDER), (ORDER, cols)]
    return (
        [pltpu.VMEM(shape, jnp.float32) for shape in given]
        + [pltpu.SemaphoreType.DMA((4,))]
        + [pltpu.VMEM(shape, jnp.bfloat16) for shape in pairs for _ in range(2)]
    )


def child_update(where, front, cols, rows, x, lower):
    kept = front.shape[0] - TILE, front.shape[1] - TILE
    return pl.pallas_call(
        child_kernel,
        out_shape=(
            jax.ShapeDtypeStruct((STEPS * STEPS, TILE, TILE), jnp.float32),
            jax.ShapeDtypeStruct((front.shape[0], TILE), jnp.float32),
        ),
        in_specs=[SMEM] + [ANY] * 4 + [VMEM],
        out_specs=(VMEM, VMEM),
        scratch_shapes=panel_scratch(*kept),
        compiler_params=pltpu.CompilerParams(vmem_limit_bytes=58 << 20),
        name="child_update",
    )(where, front, cols, rows, x, lower)


def parent_kernel(where_ref, front_ref, cols_ref, rows_ref, x_ref, lower_ref, out_ref, factor_ref, *scratch):
    x_in, cols_in, rows_in, front_in, sems = scratch[:5]
    xs, cs, rs, ls, ts = (scratch[i : i + 2] for i in range(5, 15, 2))
    col, core = where_ref[0], where_ref[1]
    copies = fetch([(x_ref, x_in), (cols_ref, cols_in), (rows_ref, rows_in), (front_ref.at[:, TILE:], front_in)], sems)
    solve_panels(col, copies, x_in, cols_in, rows_in, factor_ref, 0, xs, cs, rs, ls, ts)

    @pl.when(core == 0)
    def _():
        factor_ref[:TILE, :] = lower_ref[...]

    copies[3].wait()
    out_ref[:, :TILE] = jnp.zeros((front_in.shape[0], TILE), jnp.float32)
    for begin, width in chunks(front_in.shape[1]):
        here = slice(begin, begin + width)
        left = (ls[0][...], ls[1][...])
        out_ref[:, TILE + begin : TILE + begin + width] = front_in[:, here] - dot3(
            left, (ts[0][:, here], ts[1][:, here]), ((1,), (0,))
        )

    @pl.when(core == 0)
    def _():
        out_ref[:TILE, :] = jnp.zeros((TILE, out_ref.shape[1]), jnp.float32)


def parent_update(where, front, cols, rows, x, lower):
    return pl.pallas_call(
        parent_kernel,
        out_shape=(
            jax.ShapeDtypeStruct(front.shape, jnp.float32),
            jax.ShapeDtypeStruct((front.shape[0], TILE), jnp.float32),
        ),
        in_specs=[SMEM] + [ANY] * 4 + [VMEM],
        out_specs=(VMEM, VMEM),
        scratch_shapes=panel_scratch(front.shape[0], front.shape[1] - TILE),
        compiler_params=pltpu.CompilerParams(vmem_limit_bytes=60 << 20),
        name="parent_update",
    )(where, front, cols, rows, x, lower)


def assemble_kernel(rows_ref, cols_ref, front_ref, own_ref, other_ref, out_ref):
    tiles_row, tiles_col = (n // TILE for n in front_ref.shape)
    out_ref[...] = front_ref[...]
    for child in range(2):
        for i in range(tiles_row):
            source = rows_ref[child * tiles_row + i]

            def add(box_ref, base):
                at = slice(i * TILE, (i + 1) * TILE)
                for j in range(tiles_col):
                    place = cols_ref[child * tiles_col + j]

                    @pl.when(place >= 0)
                    def _():
                        out_ref[at, j * TILE : (j + 1) * TILE] += box_ref[base + place]

            @pl.when((source >= 0) & (source < STEPS * STEPS))
            def _():
                add(own_ref, source)

            @pl.when(source >= STEPS * STEPS)
            def _():
                add(other_ref, source - STEPS * STEPS)


def assemble(rows, cols, front, own, other):
    return pl.pallas_call(
        assemble_kernel,
        out_shape=jax.ShapeDtypeStruct(front.shape, jnp.float32),
        in_specs=[SMEM, SMEM] + [VMEM] * 3,
        out_specs=VMEM,
        compiler_params=pltpu.CompilerParams(vmem_limit_bytes=40 << 20),
        name="assemble",
    )(rows, cols, front, own, other)


def spread(x, axes):
    count = lax.axis_size(axes)
    copies = jnp.broadcast_to(x[None], (count,) + x.shape)
    return lax.all_to_all(copies, axes, 0, 0, tiled=True)


def after(x, first):
    return lax.optimization_barrier((x, first))[0]


def local(child_fronts, child_map, parent_front):
    child = lax.axis_index("sub")
    core = lax.axis_index("core")
    row = lax.axis_index(("y", "core"))
    col = lax.axis_index(COL)
    group = lax.axis_index(GROUP)
    front = child_fronts[0]
    kept = CBLK // STEPS - 1

    first = spread(front[:TILE, :TILE], "y")
    rows = lax.all_gather(after(front[:TILE, TILE:], first), ("y", "core"), axis=0, tiled=True)
    own = spread(first, COL)
    other = lax.ppermute(own, "core", SWAP)
    columns = spread(after(front[TILE:, :TILE], own), COL)
    inverse, lower = factor(jnp.stack([core, row, col]).astype(jnp.int32), own, other)
    columns = after(columns, lower)
    mine = child_map[child] // (PBLK // STEPS)
    where = jnp.concatenate(
        [
            col.reshape(1),
            lax.dynamic_slice(mine, (row * kept,), (kept,)),
            lax.dynamic_slice(mine, (col * kept,), (kept,)),
        ]
    ).astype(jnp.int32)
    box, child_factor = child_update(where, front, columns, rows, inverse, lower)

    box = lax.all_to_all(box, GROUP + COL, 0, 0, tiled=True)
    box_other = lax.ppermute(box, "core", SWAP)
    tiles_row, tiles_col = parent_front.shape[0] // TILE, parent_front.shape[1] // TILE
    blocks = jnp.arange(PBLK, dtype=jnp.int32)
    number = jnp.arange(CBLK - STEPS, dtype=jnp.int32)
    source = jnp.max(jnp.where(child_map[:, :, None] == blocks, number[:, None], -1), axis=1)
    source_row = lax.dynamic_slice(source, (0, (2 * group + core) * tiles_row), (2, tiles_row))
    source_col = lax.dynamic_slice(source, (0, col * tiles_col), (2, tiles_col))
    whose = (source_row // kept % 2 != core).astype(jnp.int32) * (STEPS * STEPS)
    place = whose + jnp.arange(2, dtype=jnp.int32)[:, None] * (STEPS * STEPS // 2) + source_row // (2 * kept) * STEPS
    place_row = jnp.where(source_row >= 0, place, -1)
    place_col = jnp.where(source_col >= 0, source_col // kept, -1)
    front = assemble(place_row.reshape(-1), place_col.reshape(-1), parent_front, box, box_other)

    down = [(0, 1)]
    half = TILE // 2
    strip = jnp.where(core == 0, front[:half, :], lax.ppermute(front[half:TILE, :], "core", down))
    rows = lax.all_gather(strip[:, TILE:], GROUP + ("core",), axis=0, tiled=True)
    own = spread(spread(strip[:, :TILE], GROUP), COL)
    other = lax.ppermute(own, "core", SWAP)
    columns = spread(after(front[:, :TILE], own), COL)
    inverse, lower = factor(jnp.stack([core, group, col]).astype(jnp.int32), own, other)
    rows, columns = after((rows, columns), lower)
    where = jnp.stack([col, core]).astype(jnp.int32)
    update, parent_factor = parent_update(where, front, columns, rows, inverse, lower)
    return (child_factor[None], parent_factor, update)


def solution(mesh):
    shape = (2, 4, 2, 2, 4)
    fine = jax.sharding.Mesh(mesh.devices.reshape(shape), ("sub", "y", "core", "xlo", "z"))
    in_specs = (P("sub", ("y", "core"), COL), P(), P(("sub", "y", "core"), COL))
    out_specs = (P("sub", ("y", "core"), COL), P(("sub", "y", "core"), COL), P(("sub", "y", "core"), COL))
    return jax.shard_map(local, mesh=fine, in_specs=in_specs, out_specs=out_specs, check_vma=False)
```

```python
import functools

import jax
import jax.numpy as jnp
from jax import lax
from jax.experimental import pallas as pl
from jax.experimental.pallas import tpu as pltpu
from jax.sharding import PartitionSpec as P

TILE = 128
STEPS = 8
CBLK = 64
PBLK = 96
ORDER = TILE * STEPS

SWAP = [(0, 1), (1, 0)]
GROUP = ("sub", "y")
COL = ("xlo", "z")
VMEM = pl.BlockSpec(memory_space=pltpu.VMEM)
SMEM = pl.BlockSpec(memory_space=pltpu.SMEM)
ANY = pl.BlockSpec(memory_space=pl.ANY)
HBM = pl.BlockSpec(memory_space=pltpu.HBM)


def split(x):
    high = x.astype(jnp.bfloat16)
    return high, (x - high.astype(jnp.float32)).astype(jnp.bfloat16)


def dot3(a, b, contract):
    dot = functools.partial(
        lax.dot_general, dimension_numbers=(contract, ((), ())), preferred_element_type=jnp.float32
    )
    return dot(a[0], b[0]) + (dot(a[0], b[1]) + dot(a[1], b[0]))


def factor_tile(s_ref, x_ref, beside):
    full = (8, TILE)
    count = TILE // 8
    lane = lax.broadcasted_iota(jnp.int32, full, 1)
    sub = lax.broadcasted_iota(jnp.int32, full, 0)
    s = [s_ref[8 * i : 8 * i + 8, :] for i in range(count)]
    for p in range(count):
        j0 = 8 * p
        inside = (lane >= j0) & (lane < j0 + 8)
        panel = s[p]
        if p == 0:
            cols = [jnp.broadcast_to(panel[:, j0 + k : j0 + k + 1], full) for k in range(8)]
        c = [[jnp.broadcast_to(cols[m][k : k + 1, :], full) if m >= k else None for m in range(8)] for k in range(8)]
        e = []
        for k in range(8):
            row = jnp.broadcast_to(panel[k : k + 1, :], full)
            e.append(jnp.where(inside, jnp.where(lane == j0 + k, 1.0, 0.0), row))
        more = p + 1 < count
        if more:
            f = [jnp.broadcast_to(s[p + 1][:, j0 + k : j0 + k + 1], full) for k in range(8)]
            later = jnp.where(inside, 0.0, s[p + 1])
            cols = [jnp.broadcast_to(s[p + 1][:, j0 + 8 + k : j0 + 9 + k], full) for k in range(8)]
        root = [None] * 8
        for k in range(8):
            root[k] = lax.rsqrt(c[k][k])
            for m in range(k, 8):
                c[k][m] = c[k][m] * root[k]
            e[k] = e[k] * root[k]
            if more:
                f[k] = f[k] * root[k]
                later = later - f[k] * e[k]
                for n in range(8):
                    cols[n] = cols[n] - f[k] * jnp.broadcast_to(f[k][n : n + 1, :], full)
            for m in range(k + 1, 8):
                for n in range(m, 8):
                    c[m][n] = c[m][n] - c[k][m] * c[k][n]
                e[m] = e[m] - c[k][m] * e[k]
                if more:
                    f[m] = f[m] - c[k][m] * f[k]
        beside(p)
        if p + 2 < count:
            q = [None] * 8
            for k in reversed(range(8)):
                row = e[k]
                for m in range(k + 1, 8):
                    row = row - c[k][m] * q[m]
                q[k] = row * root[k]
            for i in range(p + 2, count):
                new = jnp.where(inside, 0.0, s[i])
                for k in range(8):
                    new = new - jnp.broadcast_to(s[i][:, j0 + k : j0 + k + 1], full) * q[k]
                s[i] = new
        if more:
            s[p + 1] = later
        out = jnp.zeros(full, jnp.float32)
        for k in range(8):
            out = jnp.where(sub == k, e[k], out)
        x_ref[j0 : j0 + 8, :] = jnp.where(lane < j0 + 8, out, 0.0)


def factor_kernel(
    where_ref, own_ref, other_ref, high_out, rest_out, lower_ref, w_ref, u_ref, s_ref, xn_ref, xk_ref, last_ref, high_ref, rest_ref,
    x_high_ref, x_rest_ref, sems
):
    core, tile_row, tile_col = where_ref[0], where_ref[1], where_ref[2]
    groups, depth = own_ref.shape[0], own_ref.shape[2]
    pitch = ORDER // groups
    for ref, which in ((own_ref, core), (other_ref, 1 - core)):
        for g in range(groups):
            begin = pl.multiple_of(g * pitch + which * depth, depth)
            for c in range(STEPS):
                w_ref[pl.ds(begin, depth), c * TILE : (c + 1) * TILE] = ref[g, c]
    block = lax.broadcasted_iota(jnp.int32, (TILE, ORDER), 1) // TILE

    def place(k):
        return pl.ds(pl.multiple_of(k * TILE, TILE), TILE)

    def finish(k):
        row = dot3(split(xk_ref[...]), split(w_ref[place(k), :]), ((1,), (0,)))
        u_ref[place(k), :] = row
        last_ref[...] = row
        last_ref[:, place(k)] = xk_ref[...]
        row = last_ref[...]
        x_high_ref[place(k), :], x_rest_ref[place(k), :] = split(jnp.where(block <= k, row, 0.0))
        high_ref[...], rest_ref[...] = split(row)

    def leave(k):
        pairs = ((x_high_ref, high_out), (x_rest_ref, rest_out))
        return [
            pltpu.make_async_copy(source.at[place(k)], target.at[place(k)], sems.at[i, k])
            for i, (source, target) in enumerate(pairs)
        ]

    def step(k, carry):
        before = k - 1

        def beside(p):
            if p == 0:
                finish(jnp.maximum(before, 0))
            elif p % 2 == 0:
                i = p // 2
                at = slice(i * TILE, (i + 1) * TILE)
                mine = jnp.where(i > before, last_ref[:, at], 0.0).T
                held = w_ref[at, :]
                held = jnp.where((block == before) & (i > before), 0.0, held)
                w_ref[at, :] = held - dot3(split(mine), (high_ref[...], rest_ref[...]), ((1,), (0,)))

        factor_tile(s_ref, xn_ref, beside)
        xk_ref[...] = xn_ref[...]
        after_k = jnp.minimum(k + 1, STEPS - 1)
        high, rest = split(dot3(split(xn_ref[...]), split(w_ref[place(k), place(after_k)]), ((1,), (0,))))
        s_ref[...] = w_ref[place(after_k), place(after_k)] - dot3((high.T, rest.T), (high, rest), ((1,), (0,)))

        @pl.when(k > 0)
        def _():
            for copy in leave(k - 1):
                copy.start()

        return carry

    xk_ref[...] = jnp.zeros((TILE, TILE), jnp.float32)
    s_ref[...] = w_ref[:TILE, :TILE]
    lax.fori_loop(0, STEPS, step, 0)
    finish(STEPS - 1)
    for copy in leave(STEPS - 1):
        copy.start()
    order = tile_row * TILE + lax.broadcasted_iota(jnp.int32, (TILE, TILE), 1)
    upper = tile_col * TILE + lax.broadcasted_iota(jnp.int32, (TILE, TILE), 0) <= order
    lower_ref[...] = jnp.where(upper, u_ref[place(tile_col), place(tile_row)], 0.0).T
    for k in range(STEPS):
        for copy in leave(k):
            copy.wait()


def factor(where, own, other):
    return pl.pallas_call(
        factor_kernel,
        out_shape=(
            jax.ShapeDtypeStruct((ORDER, ORDER), jnp.bfloat16),
            jax.ShapeDtypeStruct((ORDER, ORDER), jnp.bfloat16),
            jax.ShapeDtypeStruct((TILE, TILE), jnp.float32),
        ),
        in_specs=[SMEM, VMEM, VMEM],
        out_specs=(HBM, HBM, VMEM),
        scratch_shapes=[pltpu.VMEM((ORDER, ORDER), jnp.float32)] * 2
        + [pltpu.VMEM((TILE, TILE), jnp.float32)] * 3
        + [pltpu.VMEM((TILE, ORDER), jnp.float32)]
        + [pltpu.VMEM((TILE, ORDER), jnp.bfloat16)] * 2
        + [pltpu.VMEM((ORDER, ORDER), jnp.bfloat16)] * 2
        + [pltpu.SemaphoreType.DMA((2, STEPS))],
        compiler_params=pltpu.CompilerParams(vmem_limit_bytes=60 << 20),
        cost_estimate=pl.CostEstimate(flops=20_000_000_000, bytes_accessed=16 << 20, transcendentals=0),
        name="factor",
    )(where, own, other)


def chunks(width):
    wide = 2 * TILE
    return [(begin, min(wide, width - begin)) for begin in range(0, width, wide)]


def fetch(pairs, sems):
    copies = [pltpu.make_async_copy(source, target, sems.at[i]) for i, (source, target) in enumerate(pairs)]
    for copy in copies:
        copy.start()
    return copies


def solve_panels(col, copies, cols_in, rows_in, factor_ref, top, xs, cs, rs, ls, ts):
    wide = 2 * TILE
    copies[0].wait()
    copies[1].wait()
    copies[2].wait()
    for c in range(STEPS):
        at = slice(c * TILE, (c + 1) * TILE)
        cs[0][:, at], cs[1][:, at] = split(cols_in[c])
    for k in range(STEPS // 2):
        depth = wide * (k + 1)
        at = slice(k * wide, depth)
        x_now = (xs[0][at, :depth], xs[1][at, :depth])
        left = dot3((cs[0][:, :depth], cs[1][:, :depth]), x_now, ((1,), (1,)))
        ls[0][:, at], ls[1][:, at] = split(left)

    mine = pl.ds(pl.multiple_of(col * TILE, TILE), TILE)
    factor_ref[top:, :] = ls[0][:, mine].astype(jnp.float32) + ls[1][:, mine].astype(jnp.float32)
    copies[3].wait()
    if len(rows_in.shape) == 2:
        rs[0][...], rs[1][...] = split(rows_in[...])
    else:
        for i in range(STEPS):
            for j in range(2):
                begin = (j * STEPS // 2 + i // 2) * TILE + i % 2 * (TILE // 2)
                at = slice(begin, begin + TILE // 2)
                rs[0][at, :], rs[1][at, :] = split(rows_in[i, j])
    for k in range(STEPS // 2):
        depth = wide * (k + 1)
        at = slice(k * wide, depth)
        x_now = (xs[0][at, :depth], xs[1][at, :depth])
        for begin, width in chunks(rows_in.shape[-1]):
            here = slice(begin, begin + width)
            right = dot3(x_now, (rs[0][:depth, here], rs[1][:depth, here]), ((1,), (0,)))
            ts[0][at, here], ts[1][at, here] = split(right)


def child_kernel(where_ref, front_ref, cols_ref, rows_ref, x_high_ref, x_rest_ref, lower_ref, box_ref, factor_ref, *scratch):
    cols_in, rows_in, front_in, sems = scratch[:4]
    xs, cs, rs, ls, ts = (scratch[i : i + 2] for i in range(4, 14, 2))
    copies = fetch(
        [(x_high_ref, xs[0]), (x_rest_ref, xs[1]), (cols_ref, cols_in), (rows_ref, rows_in), (front_ref.at[TILE:, TILE:], front_in)], sems
    )
    solve_panels(where_ref[0], copies, cols_in, rows_in, factor_ref, TILE, xs, cs, rs, ls, ts)
    factor_ref[:TILE, :] = lower_ref[...]
    copies[4].wait()
    for begin, width in chunks(front_in.shape[1]):
        here = slice(begin, begin + width)
        left = (ls[0][...], ls[1][...])
        schur = front_in[:, here] - dot3(left, (ts[0][:, here], ts[1][:, here]), ((1,), (0,)))
        for b in range(begin // TILE, (begin + width) // TILE):
            at = slice(b * TILE - begin, (b + 1) * TILE - begin)
            for a in range(STEPS - 1):
                slot = where_ref[1 + a] * STEPS + where_ref[STEPS + b]
                box_ref[slot] = schur[a * TILE : (a + 1) * TILE, at]


def panel_scratch(rows, cols, gathered):
    given = [(STEPS, rows, TILE), gathered, (rows, cols)]
    pairs = [(ORDER, ORDER), (rows, ORDER), (ORDER, cols), (rows, ORDER), (ORDER, cols)]
    return (
        [pltpu.VMEM(shape, jnp.float32) for shape in given]
        + [pltpu.SemaphoreType.DMA((5,))]
        + [pltpu.VMEM(shape, jnp.bfloat16) for shape in pairs for _ in range(2)]
    )


def child_update(where, front, cols, rows, x, lower):
    kept = front.shape[0] - TILE, front.shape[1] - TILE
    return pl.pallas_call(
        child_kernel,
        out_shape=(
            jax.ShapeDtypeStruct((STEPS * STEPS, TILE, TILE), jnp.float32),
            jax.ShapeDtypeStruct((front.shape[0], TILE), jnp.float32),
        ),
        in_specs=[SMEM] + [ANY] * 5 + [VMEM],
        out_specs=(VMEM, VMEM),
        scratch_shapes=panel_scratch(*kept, rows.shape),
        compiler_params=pltpu.CompilerParams(vmem_limit_bytes=58 << 20),
        name="child_update",
    )(where, front, cols, rows, *x, lower)


def parent_kernel(where_ref, front_ref, cols_ref, rows_ref, x_high_ref, x_rest_ref, lower_ref, out_ref, factor_ref, *scratch):
    cols_in, rows_in, front_in, sems = scratch[:4]
    xs, cs, rs, ls, ts = (scratch[i : i + 2] for i in range(4, 14, 2))
    col, core = where_ref[0], where_ref[1]
    copies = fetch([(x_high_ref, xs[0]), (x_rest_ref, xs[1]), (cols_ref, cols_in), (rows_ref, rows_in), (front_ref.at[:, TILE:], front_in)], sems)
    solve_panels(col, copies, cols_in, rows_in, factor_ref, 0, xs, cs, rs, ls, ts)

    @pl.when(core == 0)
    def _():
        factor_ref[:TILE, :] = lower_ref[...]

    copies[4].wait()
    out_ref[:, :TILE] = jnp.zeros((front_in.shape[0], TILE), jnp.float32)
    for begin, width in chunks(front_in.shape[1]):
        here = slice(begin, begin + width)
        left = (ls[0][...], ls[1][...])
        out_ref[:, TILE + begin : TILE + begin + width] = front_in[:, here] - dot3(
            left, (ts[0][:, here], ts[1][:, here]), ((1,), (0,))
        )

    @pl.when(core == 0)
    def _():
        out_ref[:TILE, :] = jnp.zeros((TILE, out_ref.shape[1]), jnp.float32)


def parent_update(where, front, cols, rows, x, lower):
    return pl.pallas_call(
        parent_kernel,
        out_shape=(
            jax.ShapeDtypeStruct(front.shape, jnp.float32),
            jax.ShapeDtypeStruct((front.shape[0], TILE), jnp.float32),
        ),
        in_specs=[SMEM] + [ANY] * 5 + [VMEM],
        out_specs=(VMEM, VMEM),
        scratch_shapes=panel_scratch(front.shape[0], front.shape[1] - TILE, rows.shape),
        compiler_params=pltpu.CompilerParams(vmem_limit_bytes=60 << 20),
        name="parent_update",
    )(where, front, cols, rows, *x, lower)


def assemble_kernel(rows_ref, cols_ref, front_ref, own_ref, other_ref, result_ref, out_ref, sems):
    tiles_row, tiles_col = (n // TILE for n in front_ref.shape)
    out_ref[...] = front_ref[...]
    def add_row(child, i, at):
        source = rows_ref[child * tiles_row + i]

        def add(box_ref, base):
            for j in range(tiles_col):
                place = cols_ref[child * tiles_col + j]

                @pl.when(place >= 0)
                def _():
                    out_ref[at, j * TILE : (j + 1) * TILE] += box_ref[base + place]

        @pl.when((source >= 0) & (source < STEPS * STEPS))
        def _():
            add(own_ref, source)

        @pl.when(source >= STEPS * STEPS)
        def _():
            add(other_ref, source - STEPS * STEPS)

    copies = []
    for i in range(tiles_row):
        at = slice(i * TILE, (i + 1) * TILE)
        for child in range(2):
            add_row(child, i, at)
        copies.append(pltpu.make_async_copy(out_ref.at[at], result_ref.at[at], sems.at[i]))
        copies[-1].start()
    for copy in copies:
        copy.wait()


def assemble(rows, cols, front, own, other):
    return pl.pallas_call(
        assemble_kernel,
        out_shape=jax.ShapeDtypeStruct(front.shape, jnp.float32),
        in_specs=[SMEM, SMEM] + [VMEM] * 3,
        out_specs=HBM,
        scratch_shapes=[pltpu.VMEM(front.shape, jnp.float32), pltpu.SemaphoreType.DMA((front.shape[0] // TILE,))],
        compiler_params=pltpu.CompilerParams(vmem_limit_bytes=60 << 20),
        name="assemble",
    )(rows, cols, front, own, other)


def spread(x, axes, first=None):
    count = lax.axis_size(axes)
    copies = jnp.broadcast_to(x[None], (count,) + x.shape)
    if first is not None:
        copies = after(copies, first)
    return lax.all_to_all(copies, axes, 0, 0, tiled=True)


def after(x, first):
    return lax.optimization_barrier((x, first))[0]


def local(child_fronts, child_map, parent_front):
    child = lax.axis_index("sub")
    core = lax.axis_index("core")
    row = lax.axis_index(("y", "core"))
    col = lax.axis_index(COL)
    group = lax.axis_index(GROUP)
    front = child_fronts[0]
    kept = CBLK // STEPS - 1

    own = spread(front[:TILE, :TILE], ("y",) + COL).reshape(-1, STEPS, TILE, TILE)
    rows = lax.all_gather(after(front[:TILE, TILE:], own), ("y", "core"), axis=0, tiled=True)
    other = lax.ppermute(own, "core", SWAP)
    columns = spread(front[TILE:, :TILE], COL, own)
    *inverse, lower = factor(jnp.stack([core, row, col]).astype(jnp.int32), own, other)
    columns = after(columns, lower)
    mine = child_map[child] // (PBLK // STEPS)
    where = jnp.concatenate(
        [
            col.reshape(1),
            lax.dynamic_slice(mine, (row * kept,), (kept,)),
            lax.dynamic_slice(mine, (col * kept,), (kept,)),
        ]
    ).astype(jnp.int32)
    box, child_factor = child_update(where, front, columns, rows, inverse, lower)

    box = lax.all_to_all(box, GROUP + COL, 0, 0, tiled=True)
    box_other = lax.ppermute(box, "core", SWAP)
    tiles_row, tiles_col = parent_front.shape[0] // TILE, parent_front.shape[1] // TILE
    blocks = jnp.arange(PBLK, dtype=jnp.int32)
    number = jnp.arange(CBLK - STEPS, dtype=jnp.int32)
    source = jnp.max(jnp.where(child_map[:, :, None] == blocks, number[:, None], -1), axis=1)
    source_row = lax.dynamic_slice(source, (0, (2 * group + core) * tiles_row), (2, tiles_row))
    source_col = lax.dynamic_slice(source, (0, col * tiles_col), (2, tiles_col))
    whose = (source_row // kept % 2 != core).astype(jnp.int32) * (STEPS * STEPS)
    place = whose + jnp.arange(2, dtype=jnp.int32)[:, None] * (STEPS * STEPS // 2) + source_row // (2 * kept) * STEPS
    place_row = jnp.where(source_row >= 0, place, -1)
    place_col = jnp.where(source_col >= 0, source_col // kept, -1)
    front = assemble(place_row.reshape(-1), place_col.reshape(-1), parent_front, box, box_other)

    down = [(0, 1)]
    half = TILE // 2
    strip = jnp.where(core == 0, front[:half, :], lax.ppermute(front[half:TILE, :], "core", down))
    strip_other = lax.ppermute(strip[:, TILE:], "sub", SWAP)
    own = spread(strip[:, :TILE], GROUP + COL).reshape(-1, STEPS, half, TILE)
    other = lax.ppermute(own, "core", SWAP)
    strip_other = after(strip_other, own)
    both = jnp.stack([jnp.where(child == i, strip[:, TILE:], strip_other) for i in range(2)])
    rows = lax.all_gather(both, ("y", "core"), axis=0)
    columns = spread(front[:, :TILE], COL, own)
    *inverse, lower = factor(jnp.stack([core, group, col]).astype(jnp.int32), own, other)
    rows, columns = after((rows, columns), lower)
    where = jnp.stack([col, core]).astype(jnp.int32)
    update, parent_factor = parent_update(where, front, columns, rows, inverse, lower)
    return (child_factor[None], parent_factor, update)


def solution(mesh):
    shape = (2, 4, 2, 2, 4)
    fine = jax.sharding.Mesh(mesh.devices.reshape(shape), ("sub", "y", "core", "xlo", "z"))
    in_specs = (P("sub", ("y", "core"), COL), P(), P(("sub", "y", "core"), COL))
    out_specs = (P("sub", ("y", "core"), COL), P(("sub", "y", "core"), COL), P(("sub", "y", "core"), COL))
    return jax.shard_map(local, mesh=fine, in_specs=in_specs, out_specs=out_specs, check_vma=False)
```

```python
import functools

import jax
import jax.numpy as jnp
from jax import lax
from jax.experimental import pallas as pl
from jax.experimental.pallas import tpu as pltpu
from jax.sharding import PartitionSpec as P

TILE = 128
STEPS = 8
CBLK = 64
PBLK = 96
ORDER = TILE * STEPS

SWAP = [(0, 1), (1, 0)]
GROUP = ("sub", "y")
COL = ("xlo", "z")
VMEM = pl.BlockSpec(memory_space=pltpu.VMEM)
SMEM = pl.BlockSpec(memory_space=pltpu.SMEM)
ANY = pl.BlockSpec(memory_space=pl.ANY)
HBM = pl.BlockSpec(memory_space=pltpu.HBM)


def split(x):
    high = x.astype(jnp.bfloat16)
    return high, (x - high.astype(jnp.float32)).astype(jnp.bfloat16)


def dot3(a, b, contract):
    dot = functools.partial(
        lax.dot_general, dimension_numbers=(contract, ((), ())), preferred_element_type=jnp.float32
    )
    return dot(a[0], b[0]) + (dot(a[0], b[1]) + dot(a[1], b[0]))


def factor_tile(s_ref, x_ref, beside):
    full = (8, TILE)
    count = TILE // 8
    lane = lax.broadcasted_iota(jnp.int32, full, 1)
    sub = lax.broadcasted_iota(jnp.int32, full, 0)
    s = [s_ref[8 * i : 8 * i + 8, :] for i in range(count)]
    for p in range(count):
        j0 = 8 * p
        inside = (lane >= j0) & (lane < j0 + 8)
        panel = s[p]
        if p == 0:
            cols = [jnp.broadcast_to(panel[:, j0 + k : j0 + k + 1], full) for k in range(8)]
        c = [[jnp.broadcast_to(cols[m][k : k + 1, :], full) if m >= k else None for m in range(8)] for k in range(8)]
        e = []
        for k in range(8):
            row = jnp.broadcast_to(panel[k : k + 1, :], full)
            e.append(jnp.where(inside, jnp.where(lane == j0 + k, 1.0, 0.0), row))
        more = p + 1 < count
        if more:
            f = [jnp.broadcast_to(s[p + 1][:, j0 + k : j0 + k + 1], full) for k in range(8)]
            later = jnp.where(inside, 0.0, s[p + 1])
            cols = [jnp.broadcast_to(s[p + 1][:, j0 + 8 + k : j0 + 9 + k], full) for k in range(8)]
        root = [None] * 8
        for k in range(8):
            root[k] = lax.rsqrt(c[k][k])
            for m in range(k, 8):
                c[k][m] = c[k][m] * root[k]
            e[k] = e[k] * root[k]
            if more:
                f[k] = f[k] * root[k]
                later = later - f[k] * e[k]
                for n in range(8):
                    cols[n] = cols[n] - f[k] * jnp.broadcast_to(f[k][n : n + 1, :], full)
            for m in range(k + 1, 8):
                for n in range(m, 8):
                    c[m][n] = c[m][n] - c[k][m] * c[k][n]
                e[m] = e[m] - c[k][m] * e[k]
                if more:
                    f[m] = f[m] - c[k][m] * f[k]
        beside(p)
        if p + 2 < count:
            q = [None] * 8
            for k in reversed(range(8)):
                row = e[k]
                for m in range(k + 1, 8):
                    row = row - c[k][m] * q[m]
                q[k] = row * root[k]
            for i in range(p + 2, count):
                new = jnp.where(inside, 0.0, s[i])
                for k in range(8):
                    new = new - jnp.broadcast_to(s[i][:, j0 + k : j0 + k + 1], full) * q[k]
                s[i] = new
        if more:
            s[p + 1] = later
        out = jnp.zeros(full, jnp.float32)
        for k in range(8):
            out = jnp.where(sub == k, e[k], out)
        x_ref[j0 : j0 + 8, :] = jnp.where(lane < j0 + 8, out, 0.0)


def pack(tile, row, col):
    half = TILE // 2
    at = lax.broadcasted_iota(jnp.int32, (half, half), 0) - lax.broadcasted_iota(jnp.int32, (half, half), 1)
    corner = tile[half:, half:]
    mixed = jnp.concatenate([jnp.where(at > 0, corner, tile[:half, :half]), tile[:half, half:]], 1)
    body = jnp.where(row == col, mixed, jnp.where(row < col, tile[:half], tile[:, half:].T))
    middle = jnp.sum(jnp.where(at == 0, corner, 0.0), axis=0, keepdims=True)
    return jnp.concatenate([body, jnp.pad(middle, ((0, 15), (0, half)))], 0)


def unpack(refs, w_ref):
    half = TILE // 2
    groups = refs[0].shape[0]
    lane = lax.broadcasted_iota(jnp.int32, (TILE, TILE), 1)
    sub = lax.broadcasted_iota(jnp.int32, (TILE, TILE), 0)
    for r in range(STEPS):
        for c in range(STEPS):
            if groups < STEPS:
                piece = refs[r % 2][r // 2, c]
            else:
                piece = jnp.concatenate([refs[0][r, c], refs[1][r, c]], 0)
            body = piece[:half]
            if r < c:
                w_ref[r * TILE : r * TILE + half, c * TILE : (c + 1) * TILE] = body
            elif r > c:
                w_ref[c * TILE + half : (c + 1) * TILE, r * TILE : (r + 1) * TILE] = body
            else:
                turned = jnp.concatenate([body, jnp.zeros((half, TILE), jnp.float32)], 0).T[:half]
                middle = jnp.broadcast_to(piece[half : half + 1], (half, TILE))
                order = lane[:half] - sub[:half]
                low = jnp.where(order == 0, middle, jnp.where(order > 0, turned, 0.0))
                low = jnp.where(lane[:half] >= half, pltpu.roll(jnp.where(lane[:half] < half, low, 0.0), half, 1), 0.0)
                whole = jnp.concatenate([body, low], 0)
                w_ref[r * TILE : (r + 1) * TILE, r * TILE : (r + 1) * TILE] = jnp.where(lane >= sub, whole, whole.T)


def factor_kernel(
    where_ref, own_ref, other_ref, high_out, rest_out, lower_ref, w_ref, u_ref, s_ref, xn_ref, xk_ref, last_ref, high_ref, rest_ref,
    x_high_ref, x_rest_ref, sems
):
    core, tile_row, tile_col = where_ref[0], where_ref[1], where_ref[2]

    @pl.when(core == 0)
    def _():
        unpack((own_ref, other_ref), w_ref)

    @pl.when(core == 1)
    def _():
        unpack((other_ref, own_ref), w_ref)

    block = lax.broadcasted_iota(jnp.int32, (TILE, ORDER), 1) // TILE

    def place(k):
        return pl.ds(pl.multiple_of(k * TILE, TILE), TILE)

    def finish(k):
        row = dot3(split(xk_ref[...]), split(w_ref[place(k), :]), ((1,), (0,)))
        u_ref[place(k), :] = row
        last_ref[...] = row
        last_ref[:, place(k)] = xk_ref[...]
        row = last_ref[...]
        x_high_ref[place(k), :], x_rest_ref[place(k), :] = split(jnp.where(block <= k, row, 0.0))
        high_ref[...], rest_ref[...] = split(row)

    def leave(k):
        pairs = ((x_high_ref, high_out), (x_rest_ref, rest_out))
        return [
            pltpu.make_async_copy(source.at[place(k)], target.at[place(k)], sems.at[i, k])
            for i, (source, target) in enumerate(pairs)
        ]

    def step(k, carry):
        before = k - 1

        def beside(p):
            if p == 0:
                finish(jnp.maximum(before, 0))
            elif p % 2 == 0:
                i = p // 2
                at = slice(i * TILE, (i + 1) * TILE)
                mine = jnp.where(i > before, last_ref[:, at], 0.0).T
                held = w_ref[at, :]
                held = jnp.where((block == before) & (i > before), 0.0, held)
                w_ref[at, :] = held - dot3(split(mine), (high_ref[...], rest_ref[...]), ((1,), (0,)))

        factor_tile(s_ref, xn_ref, beside)
        xk_ref[...] = xn_ref[...]
        after_k = jnp.minimum(k + 1, STEPS - 1)
        high, rest = split(dot3(split(xn_ref[...]), split(w_ref[place(k), place(after_k)]), ((1,), (0,))))
        s_ref[...] = w_ref[place(after_k), place(after_k)] - dot3((high.T, rest.T), (high, rest), ((1,), (0,)))

        @pl.when(k > 0)
        def _():
            for copy in leave(k - 1):
                copy.start()

        return carry

    xk_ref[...] = jnp.zeros((TILE, TILE), jnp.float32)
    s_ref[...] = w_ref[:TILE, :TILE]
    lax.fori_loop(0, STEPS, step, 0)
    finish(STEPS - 1)
    for copy in leave(STEPS - 1):
        copy.start()
    order = tile_row * TILE + lax.broadcasted_iota(jnp.int32, (TILE, TILE), 1)
    upper = tile_col * TILE + lax.broadcasted_iota(jnp.int32, (TILE, TILE), 0) <= order
    lower_ref[...] = jnp.where(upper, u_ref[place(tile_col), place(tile_row)], 0.0).T
    for k in range(STEPS):
        for copy in leave(k):
            copy.wait()


def factor(where, own, other):
    return pl.pallas_call(
        factor_kernel,
        out_shape=(
            jax.ShapeDtypeStruct((ORDER, ORDER), jnp.bfloat16),
            jax.ShapeDtypeStruct((ORDER, ORDER), jnp.bfloat16),
            jax.ShapeDtypeStruct((TILE, TILE), jnp.float32),
        ),
        in_specs=[SMEM, VMEM, VMEM],
        out_specs=(HBM, HBM, VMEM),
        scratch_shapes=[pltpu.VMEM((ORDER, ORDER), jnp.float32)] * 2
        + [pltpu.VMEM((TILE, TILE), jnp.float32)] * 3
        + [pltpu.VMEM((TILE, ORDER), jnp.float32)]
        + [pltpu.VMEM((TILE, ORDER), jnp.bfloat16)] * 2
        + [pltpu.VMEM((ORDER, ORDER), jnp.bfloat16)] * 2
        + [pltpu.SemaphoreType.DMA((2, STEPS))],
        compiler_params=pltpu.CompilerParams(vmem_limit_bytes=60 << 20),
        cost_estimate=pl.CostEstimate(flops=20_000_000_000, bytes_accessed=16 << 20, transcendentals=0),
        name="factor",
    )(where, own, other)


def chunks(width):
    wide = 2 * TILE
    return [(begin, min(wide, width - begin)) for begin in range(0, width, wide)]


def fetch(pairs, sems):
    copies = [pltpu.make_async_copy(source, target, sems.at[i]) for i, (source, target) in enumerate(pairs)]
    for copy in copies:
        copy.start()
    return copies


def solve_panels(col, copies, cols_in, rows_in, factor_ref, top, xs, cs, rs, ls, ts):
    wide = 2 * TILE
    copies[0].wait()
    copies[1].wait()
    copies[2].wait()
    for c in range(STEPS):
        at = slice(c * TILE, (c + 1) * TILE)
        cs[0][:, at], cs[1][:, at] = split(cols_in[c])
    for k in range(STEPS // 2):
        depth = wide * (k + 1)
        at = slice(k * wide, depth)
        x_now = (xs[0][at, :depth], xs[1][at, :depth])
        left = dot3((cs[0][:, :depth], cs[1][:, :depth]), x_now, ((1,), (1,)))
        ls[0][:, at], ls[1][:, at] = split(left)

    mine = pl.ds(pl.multiple_of(col * TILE, TILE), TILE)
    factor_ref[top:, :] = ls[0][:, mine].astype(jnp.float32) + ls[1][:, mine].astype(jnp.float32)
    copies[3].wait()
    if len(rows_in.shape) == 2:
        rs[0][...], rs[1][...] = split(rows_in[...])
    else:
        for i in range(STEPS):
            for j in range(2):
                begin = (j * STEPS // 2 + i // 2) * TILE + i % 2 * (TILE // 2)
                at = slice(begin, begin + TILE // 2)
                rs[0][at, :], rs[1][at, :] = split(rows_in[i, j])
    for k in range(STEPS // 2):
        depth = wide * (k + 1)
        at = slice(k * wide, depth)
        x_now = (xs[0][at, :depth], xs[1][at, :depth])
        for begin, width in chunks(rows_in.shape[-1]):
            here = slice(begin, begin + width)
            right = dot3(x_now, (rs[0][:depth, here], rs[1][:depth, here]), ((1,), (0,)))
            ts[0][at, here], ts[1][at, here] = split(right)


def child_kernel(where_ref, front_ref, cols_ref, rows_ref, x_high_ref, x_rest_ref, lower_ref, box_ref, factor_ref, *scratch):
    cols_in, rows_in, front_in, sems = scratch[:4]
    xs, cs, rs, ls, ts = (scratch[i : i + 2] for i in range(4, 14, 2))
    copies = fetch(
        [(x_high_ref, xs[0]), (x_rest_ref, xs[1]), (cols_ref, cols_in), (rows_ref, rows_in), (front_ref.at[TILE:, TILE:], front_in)], sems
    )
    solve_panels(where_ref[0], copies, cols_in, rows_in, factor_ref, TILE, xs, cs, rs, ls, ts)
    factor_ref[:TILE, :] = lower_ref[...]
    copies[4].wait()
    for begin, width in chunks(front_in.shape[1]):
        here = slice(begin, begin + width)
        left = (ls[0][...], ls[1][...])
        schur = front_in[:, here] - dot3(left, (ts[0][:, here], ts[1][:, here]), ((1,), (0,)))
        for b in range(begin // TILE, (begin + width) // TILE):
            at = slice(b * TILE - begin, (b + 1) * TILE - begin)
            for a in range(STEPS - 1):
                slot = where_ref[1 + a] * STEPS + where_ref[STEPS + b]
                box_ref[slot] = schur[a * TILE : (a + 1) * TILE, at]


def panel_scratch(rows, cols, gathered):
    given = [(STEPS, rows, TILE), gathered, (rows, cols)]
    pairs = [(ORDER, ORDER), (rows, ORDER), (ORDER, cols), (rows, ORDER), (ORDER, cols)]
    return (
        [pltpu.VMEM(shape, jnp.float32) for shape in given]
        + [pltpu.SemaphoreType.DMA((5,))]
        + [pltpu.VMEM(shape, jnp.bfloat16) for shape in pairs for _ in range(2)]
    )


def child_update(where, front, cols, rows, x, lower):
    kept = front.shape[0] - TILE, front.shape[1] - TILE
    return pl.pallas_call(
        child_kernel,
        out_shape=(
            jax.ShapeDtypeStruct((STEPS * STEPS, TILE, TILE), jnp.float32),
            jax.ShapeDtypeStruct((front.shape[0], TILE), jnp.float32),
        ),
        in_specs=[SMEM] + [ANY] * 5 + [VMEM],
        out_specs=(VMEM, VMEM),
        scratch_shapes=panel_scratch(*kept, rows.shape),
        compiler_params=pltpu.CompilerParams(vmem_limit_bytes=58 << 20),
        name="child_update",
    )(where, front, cols, rows, *x, lower)


def parent_kernel(where_ref, front_ref, cols_ref, rows_ref, x_high_ref, x_rest_ref, lower_ref, out_ref, factor_ref, *scratch):
    cols_in, rows_in, front_in, sems = scratch[:4]
    xs, cs, rs, ls, ts = (scratch[i : i + 2] for i in range(4, 14, 2))
    col, core = where_ref[0], where_ref[1]
    copies = fetch([(x_high_ref, xs[0]), (x_rest_ref, xs[1]), (cols_ref, cols_in), (rows_ref, rows_in), (front_ref.at[:, TILE:], front_in)], sems)
    solve_panels(col, copies, cols_in, rows_in, factor_ref, 0, xs, cs, rs, ls, ts)

    @pl.when(core == 0)
    def _():
        factor_ref[:TILE, :] = lower_ref[...]

    copies[4].wait()
    out_ref[:, :TILE] = jnp.zeros((front_in.shape[0], TILE), jnp.float32)
    for begin, width in chunks(front_in.shape[1]):
        here = slice(begin, begin + width)
        left = (ls[0][...], ls[1][...])
        out_ref[:, TILE + begin : TILE + begin + width] = front_in[:, here] - dot3(
            left, (ts[0][:, here], ts[1][:, here]), ((1,), (0,))
        )

    @pl.when(core == 0)
    def _():
        out_ref[:TILE, :] = jnp.zeros((TILE, out_ref.shape[1]), jnp.float32)


def parent_update(where, front, cols, rows, x, lower):
    return pl.pallas_call(
        parent_kernel,
        out_shape=(
            jax.ShapeDtypeStruct(front.shape, jnp.float32),
            jax.ShapeDtypeStruct((front.shape[0], TILE), jnp.float32),
        ),
        in_specs=[SMEM] + [ANY] * 5 + [VMEM],
        out_specs=(VMEM, VMEM),
        scratch_shapes=panel_scratch(front.shape[0], front.shape[1] - TILE, rows.shape),
        compiler_params=pltpu.CompilerParams(vmem_limit_bytes=60 << 20),
        name="parent_update",
    )(where, front, cols, rows, *x, lower)


def assemble_kernel(rows_ref, cols_ref, front_ref, own_ref, other_ref, result_ref, out_ref, sems):
    tiles_row, tiles_col = (n // TILE for n in front_ref.shape)
    out_ref[...] = front_ref[...]
    def add_row(child, i, at):
        source = rows_ref[child * tiles_row + i]

        def add(box_ref, base):
            for j in range(tiles_col):
                place = cols_ref[child * tiles_col + j]

                @pl.when(place >= 0)
                def _():
                    out_ref[at, j * TILE : (j + 1) * TILE] += box_ref[base + place]

        @pl.when((source >= 0) & (source < STEPS * STEPS))
        def _():
            add(own_ref, source)

        @pl.when(source >= STEPS * STEPS)
        def _():
            add(other_ref, source - STEPS * STEPS)

    copies = []
    for i in range(tiles_row):
        at = slice(i * TILE, (i + 1) * TILE)
        for child in range(2):
            add_row(child, i, at)
        copies.append(pltpu.make_async_copy(out_ref.at[at], result_ref.at[at], sems.at[i]))
        copies[-1].start()
    for copy in copies:
        copy.wait()


def assemble(rows, cols, front, own, other):
    return pl.pallas_call(
        assemble_kernel,
        out_shape=jax.ShapeDtypeStruct(front.shape, jnp.float32),
        in_specs=[SMEM, SMEM] + [VMEM] * 3,
        out_specs=HBM,
        scratch_shapes=[pltpu.VMEM(front.shape, jnp.float32), pltpu.SemaphoreType.DMA((front.shape[0] // TILE,))],
        compiler_params=pltpu.CompilerParams(vmem_limit_bytes=60 << 20),
        name="assemble",
    )(rows, cols, front, own, other)


def spread(x, axes, first=None):
    count = lax.axis_size(axes)
    copies = jnp.broadcast_to(x[None], (count,) + x.shape)
    if first is not None:
        copies = after(copies, first)
    return lax.all_to_all(copies, axes, 0, 0, tiled=True)


def after(x, first):
    return lax.optimization_barrier((x, first))[0]


def local(child_fronts, child_map, parent_front):
    child = lax.axis_index("sub")
    core = lax.axis_index("core")
    row = lax.axis_index(("y", "core"))
    col = lax.axis_index(COL)
    group = lax.axis_index(GROUP)
    front = child_fronts[0]
    kept = CBLK // STEPS - 1

    piece = pack(front[:TILE, :TILE], row, col)[:72]
    own = spread(piece, ("y",) + COL).reshape((-1, STEPS) + piece.shape)
    rows = lax.all_gather(after(front[:TILE, TILE:], own), ("y", "core"), axis=0, tiled=True)
    other = lax.ppermute(own, "core", SWAP)
    columns = spread(front[TILE:, :TILE], COL, own)
    *inverse, lower = factor(jnp.stack([core, row, col]).astype(jnp.int32), own, other)
    columns = after(columns, lower)
    mine = child_map[child] // (PBLK // STEPS)
    where = jnp.concatenate(
        [
            col.reshape(1),
            lax.dynamic_slice(mine, (row * kept,), (kept,)),
            lax.dynamic_slice(mine, (col * kept,), (kept,)),
        ]
    ).astype(jnp.int32)
    box, child_factor = child_update(where, front, columns, rows, inverse, lower)

    box = lax.all_to_all(box, GROUP + COL, 0, 0, tiled=True)
    box_other = lax.ppermute(box, "core", SWAP)
    tiles_row, tiles_col = parent_front.shape[0] // TILE, parent_front.shape[1] // TILE
    blocks = jnp.arange(PBLK, dtype=jnp.int32)
    number = jnp.arange(CBLK - STEPS, dtype=jnp.int32)
    source = jnp.max(jnp.where(child_map[:, :, None] == blocks, number[:, None], -1), axis=1)
    source_row = lax.dynamic_slice(source, (0, (2 * group + core) * tiles_row), (2, tiles_row))
    source_col = lax.dynamic_slice(source, (0, col * tiles_col), (2, tiles_col))
    whose = (source_row // kept % 2 != core).astype(jnp.int32) * (STEPS * STEPS)
    place = whose + jnp.arange(2, dtype=jnp.int32)[:, None] * (STEPS * STEPS // 2) + source_row // (2 * kept) * STEPS
    place_row = jnp.where(source_row >= 0, place, -1)
    place_col = jnp.where(source_col >= 0, source_col // kept, -1)
    front = assemble(place_row.reshape(-1), place_col.reshape(-1), parent_front, box, box_other)

    down = [(0, 1)]
    half = TILE // 2
    strip = jnp.where(core == 0, front[:half, :], lax.ppermute(front[half:TILE, :], "core", down))
    strip_other = lax.ppermute(strip[:, TILE:], "sub", SWAP)
    piece = pack(front[:TILE, :TILE], group, col)
    part = piece.shape[0] // 2
    piece = jnp.where(core == 0, piece[:part], lax.ppermute(piece[part:], "core", down))
    own = spread(piece, GROUP + COL).reshape((-1, STEPS) + piece.shape)
    other = lax.ppermute(own, "core", SWAP)
    strip_other = after(strip_other, own)
    both = jnp.stack([jnp.where(child == i, strip[:, TILE:], strip_other) for i in range(2)])
    rows = lax.all_gather(both, ("y", "core"), axis=0)
    columns = spread(front[:, :TILE], COL, own)
    *inverse, lower = factor(jnp.stack([core, group, col]).astype(jnp.int32), own, other)
    rows, columns = after((rows, columns), lower)
    where = jnp.stack([col, core]).astype(jnp.int32)
    update, parent_factor = parent_update(where, front, columns, rows, inverse, lower)
    return (child_factor[None], parent_factor, update)


def solution(mesh):
    shape = (2, 4, 2, 2, 4)
    fine = jax.sharding.Mesh(mesh.devices.reshape(shape), ("sub", "y", "core", "xlo", "z"))
    in_specs = (P("sub", ("y", "core"), COL), P(), P(("sub", "y", "core"), COL))
    out_specs = (P("sub", ("y", "core"), COL), P(("sub", "y", "core"), COL), P(("sub", "y", "core"), COL))
    return jax.shard_map(local, mesh=fine, in_specs=in_specs, out_specs=out_specs, check_vma=False)
```

```python
import functools

import jax
import jax.numpy as jnp
from jax import lax
from jax.experimental import pallas as pl
from jax.experimental.pallas import tpu as pltpu
from jax.sharding import PartitionSpec as P

TILE = 128
STEPS = 8
CBLK = 64
PBLK = 96
ORDER = TILE * STEPS

SWAP = [(0, 1), (1, 0)]
GROUP = ("sub", "y")
COL = ("xlo", "z")
VMEM = pl.BlockSpec(memory_space=pltpu.VMEM)
SMEM = pl.BlockSpec(memory_space=pltpu.SMEM)
ANY = pl.BlockSpec(memory_space=pl.ANY)
HBM = pl.BlockSpec(memory_space=pltpu.HBM)


def split(x):
    high = x.astype(jnp.bfloat16)
    return high, (x - high.astype(jnp.float32)).astype(jnp.bfloat16)


def dot3(a, b, contract):
    dot = functools.partial(
        lax.dot_general, dimension_numbers=(contract, ((), ())), preferred_element_type=jnp.float32
    )
    return dot(a[0], b[0]) + (dot(a[0], b[1]) + dot(a[1], b[0]))


def factor_tile(s_ref, x_ref, beside):
    full = (8, TILE)
    count = TILE // 8
    lane = lax.broadcasted_iota(jnp.int32, full, 1)
    sub = lax.broadcasted_iota(jnp.int32, full, 0)
    s = [s_ref[8 * i : 8 * i + 8, :] for i in range(count)]
    for p in range(count):
        j0 = 8 * p
        inside = (lane >= j0) & (lane < j0 + 8)
        panel = s[p]
        if p == 0:
            cols = [jnp.broadcast_to(panel[:, j0 + k : j0 + k + 1], full) for k in range(8)]
        c = [[jnp.broadcast_to(cols[m][k : k + 1, :], full) if m >= k else None for m in range(8)] for k in range(8)]
        e = []
        for k in range(8):
            row = jnp.broadcast_to(panel[k : k + 1, :], full)
            e.append(jnp.where(inside, jnp.where(lane == j0 + k, 1.0, 0.0), row))
        more = p + 1 < count
        if more:
            f = [jnp.broadcast_to(s[p + 1][:, j0 + k : j0 + k + 1], full) for k in range(8)]
            later = jnp.where(inside, 0.0, s[p + 1])
            cols = [jnp.broadcast_to(s[p + 1][:, j0 + 8 + k : j0 + 9 + k], full) for k in range(8)]
        root = [None] * 8
        for k in range(8):
            root[k] = lax.rsqrt(c[k][k])
            for m in range(k, 8):
                c[k][m] = c[k][m] * root[k]
            e[k] = e[k] * root[k]
            if more:
                f[k] = f[k] * root[k]
                later = later - f[k] * e[k]
                for n in range(8):
                    cols[n] = cols[n] - f[k] * jnp.broadcast_to(f[k][n : n + 1, :], full)
            for m in range(k + 1, 8):
                for n in range(m, 8):
                    c[m][n] = c[m][n] - c[k][m] * c[k][n]
                e[m] = e[m] - c[k][m] * e[k]
                if more:
                    f[m] = f[m] - c[k][m] * f[k]
        beside(p)
        if p + 2 < count:
            q = [None] * 8
            for k in reversed(range(8)):
                row = e[k]
                for m in range(k + 1, 8):
                    row = row - c[k][m] * q[m]
                q[k] = row * root[k]
            near = p + 3 + (count - p - 3) % 2
            for i in range(p + 2, min(near, count)):
                new = jnp.where(inside, 0.0, s[i])
                for k in range(8):
                    new = new - jnp.broadcast_to(s[i][:, j0 + k : j0 + k + 1], full) * q[k]
                s[i] = new
            if near < count:
                eight = jnp.zeros(full, jnp.float32)
                for k in range(8):
                    eight = jnp.where(sub == k, q[k], eight)
                zeros = [jnp.zeros((j0, TILE), jnp.float32)] if p else []
                right = jnp.concatenate(zeros + [eight, jnp.zeros((TILE - 8 - j0, TILE), jnp.float32)], 0)
                rest = jnp.concatenate(s[near:], 0)
                within = jnp.concatenate([inside] * (count - near), 0)
                product = dot3(split(jnp.where(within, rest, 0.0)), split(right), ((1,), (0,)))
                rest = jnp.where(within, 0.0, rest) - product
                for i in range(near, count):
                    s[i] = rest[8 * (i - near) : 8 * (i - near) + 8]
        if more:
            s[p + 1] = later
        out = jnp.zeros(full, jnp.float32)
        for k in range(8):
            out = jnp.where(sub == k, e[k], out)
        x_ref[j0 : j0 + 8, :] = jnp.where(lane < j0 + 8, out, 0.0)


def pack(tile, row, col):
    half = TILE // 2
    at = lax.broadcasted_iota(jnp.int32, (half, half), 0) - lax.broadcasted_iota(jnp.int32, (half, half), 1)
    corner = tile[half:, half:]
    mixed = jnp.concatenate([jnp.where(at > 0, corner, tile[:half, :half]), tile[:half, half:]], 1)
    body = jnp.where(row == col, mixed, jnp.where(row < col, tile[:half], tile[:, half:].T))
    middle = jnp.sum(jnp.where(at == 0, corner, 0.0), axis=0, keepdims=True)
    return jnp.concatenate([body, jnp.pad(middle, ((0, 15), (0, half)))], 0)


def unpack(refs, w_ref):
    half = TILE // 2
    groups = refs[0].shape[0]
    lane = lax.broadcasted_iota(jnp.int32, (TILE, TILE), 1)
    sub = lax.broadcasted_iota(jnp.int32, (TILE, TILE), 0)
    for r in range(STEPS):
        for c in range(STEPS):
            if groups < STEPS:
                piece = refs[r % 2][r // 2, c]
            else:
                piece = jnp.concatenate([refs[0][r, c], refs[1][r, c]], 0)
            body = piece[:half]
            if r < c:
                w_ref[r * TILE : r * TILE + half, c * TILE : (c + 1) * TILE] = body
            elif r > c:
                w_ref[c * TILE + half : (c + 1) * TILE, r * TILE : (r + 1) * TILE] = body
            else:
                turned = jnp.concatenate([body, jnp.zeros((half, TILE), jnp.float32)], 0).T[:half]
                middle = jnp.broadcast_to(piece[half : half + 1], (half, TILE))
                order = lane[:half] - sub[:half]
                low = jnp.where(order == 0, middle, jnp.where(order > 0, turned, 0.0))
                low = jnp.where(lane[:half] >= half, pltpu.roll(jnp.where(lane[:half] < half, low, 0.0), half, 1), 0.0)
                whole = jnp.concatenate([body, low], 0)
                w_ref[r * TILE : (r + 1) * TILE, r * TILE : (r + 1) * TILE] = jnp.where(lane >= sub, whole, whole.T)


def factor_kernel(
    where_ref, own_ref, other_ref, high_out, rest_out, lower_ref, w_ref, u_ref, s_ref, xn_ref, xk_ref, last_ref, high_ref, rest_ref,
    x_high_ref, x_rest_ref, sems
):
    core, tile_row, tile_col = where_ref[0], where_ref[1], where_ref[2]

    @pl.when(core == 0)
    def _():
        unpack((own_ref, other_ref), w_ref)

    @pl.when(core == 1)
    def _():
        unpack((other_ref, own_ref), w_ref)

    block = lax.broadcasted_iota(jnp.int32, (TILE, ORDER), 1) // TILE

    def place(k):
        return pl.ds(pl.multiple_of(k * TILE, TILE), TILE)

    def finish(k):
        row = dot3(split(xk_ref[...]), split(w_ref[place(k), :]), ((1,), (0,)))
        u_ref[place(k), :] = row
        last_ref[...] = row
        last_ref[:, place(k)] = xk_ref[...]
        row = last_ref[...]
        x_high_ref[place(k), :], x_rest_ref[place(k), :] = split(jnp.where(block <= k, row, 0.0))
        high_ref[...], rest_ref[...] = split(row)

    def leave(k):
        pairs = ((x_high_ref, high_out), (x_rest_ref, rest_out))
        return [
            pltpu.make_async_copy(source.at[place(k)], target.at[place(k)], sems.at[i, k])
            for i, (source, target) in enumerate(pairs)
        ]

    def step(k, carry):
        before = k - 1

        def beside(p):
            if p == 0:
                finish(jnp.maximum(before, 0))
            elif p % 2 == 0:
                i = p // 2
                at = slice(i * TILE, (i + 1) * TILE)
                mine = jnp.where(i > before, last_ref[:, at], 0.0).T
                held = w_ref[at, :]
                held = jnp.where((block == before) & (i > before), 0.0, held)
                w_ref[at, :] = held - dot3(split(mine), (high_ref[...], rest_ref[...]), ((1,), (0,)))

        factor_tile(s_ref, xn_ref, beside)
        xk_ref[...] = xn_ref[...]
        after_k = jnp.minimum(k + 1, STEPS - 1)
        high, rest = split(dot3(split(xn_ref[...]), split(w_ref[place(k), place(after_k)]), ((1,), (0,))))
        s_ref[...] = w_ref[place(after_k), place(after_k)] - dot3((high.T, rest.T), (high, rest), ((1,), (0,)))

        @pl.when(k > 0)
        def _():
            for copy in leave(k - 1):
                copy.start()

        return carry

    xk_ref[...] = jnp.zeros((TILE, TILE), jnp.float32)
    s_ref[...] = w_ref[:TILE, :TILE]
    lax.fori_loop(0, STEPS, step, 0)
    finish(STEPS - 1)
    for copy in leave(STEPS - 1):
        copy.start()
    order = tile_row * TILE + lax.broadcasted_iota(jnp.int32, (TILE, TILE), 1)
    upper = tile_col * TILE + lax.broadcasted_iota(jnp.int32, (TILE, TILE), 0) <= order
    lower_ref[...] = jnp.where(upper, u_ref[place(tile_col), place(tile_row)], 0.0).T
    for k in range(STEPS):
        for copy in leave(k):
            copy.wait()


def factor(where, own, other):
    return pl.pallas_call(
        factor_kernel,
        out_shape=(
            jax.ShapeDtypeStruct((ORDER, ORDER), jnp.bfloat16),
            jax.ShapeDtypeStruct((ORDER, ORDER), jnp.bfloat16),
            jax.ShapeDtypeStruct((TILE, TILE), jnp.float32),
        ),
        in_specs=[SMEM, VMEM, VMEM],
        out_specs=(HBM, HBM, VMEM),
        scratch_shapes=[pltpu.VMEM((ORDER, ORDER), jnp.float32)] * 2
        + [pltpu.VMEM((TILE, TILE), jnp.float32)] * 3
        + [pltpu.VMEM((TILE, ORDER), jnp.float32)]
        + [pltpu.VMEM((TILE, ORDER), jnp.bfloat16)] * 2
        + [pltpu.VMEM((ORDER, ORDER), jnp.bfloat16)] * 2
        + [pltpu.SemaphoreType.DMA((2, STEPS))],
        compiler_params=pltpu.CompilerParams(vmem_limit_bytes=60 << 20),
        cost_estimate=pl.CostEstimate(flops=20_000_000_000, bytes_accessed=16 << 20, transcendentals=0),
        name="factor",
    )(where, own, other)


def chunks(width):
    wide = 2 * TILE
    return [(begin, min(wide, width - begin)) for begin in range(0, width, wide)]


def fetch(pairs, sems):
    copies = [pltpu.make_async_copy(source, target, sems.at[i]) for i, (source, target) in enumerate(pairs)]
    for copy in copies:
        copy.start()
    return copies


def solve_panels(col, copies, cols_in, rows_in, factor_ref, top, xs, cs, rs, ls, ts):
    wide = 2 * TILE
    copies[0].wait()
    copies[1].wait()
    copies[2].wait()
    for c in range(STEPS):
        at = slice(c * TILE, (c + 1) * TILE)
        cs[0][:, at], cs[1][:, at] = split(cols_in[c])
    for k in range(STEPS // 2):
        depth = wide * (k + 1)
        at = slice(k * wide, depth)
        x_now = (xs[0][at, :depth], xs[1][at, :depth])
        left = dot3((cs[0][:, :depth], cs[1][:, :depth]), x_now, ((1,), (1,)))
        ls[0][:, at], ls[1][:, at] = split(left)

    mine = pl.ds(pl.multiple_of(col * TILE, TILE), TILE)
    factor_ref[top:, :] = ls[0][:, mine].astype(jnp.float32) + ls[1][:, mine].astype(jnp.float32)
    copies[3].wait()
    if len(rows_in.shape) == 2:
        rs[0][...], rs[1][...] = split(rows_in[...])
    else:
        for i in range(STEPS):
            for j in range(2):
                begin = (j * STEPS // 2 + i // 2) * TILE + i % 2 * (TILE // 2)
                at = slice(begin, begin + TILE // 2)
                rs[0][at, :], rs[1][at, :] = split(rows_in[i, j])
    for k in range(STEPS // 2):
        depth = wide * (k + 1)
        at = slice(k * wide, depth)
        x_now = (xs[0][at, :depth], xs[1][at, :depth])
        for begin, width in chunks(rows_in.shape[-1]):
            here = slice(begin, begin + width)
            right = dot3(x_now, (rs[0][:depth, here], rs[1][:depth, here]), ((1,), (0,)))
            ts[0][at, here], ts[1][at, here] = split(right)


def child_kernel(where_ref, front_ref, cols_ref, rows_ref, x_high_ref, x_rest_ref, lower_ref, box_ref, factor_ref, *scratch):
    cols_in, rows_in, front_in, sems = scratch[:4]
    xs, cs, rs, ls, ts = (scratch[i : i + 2] for i in range(4, 14, 2))
    copies = fetch(
        [(x_high_ref, xs[0]), (x_rest_ref, xs[1]), (cols_ref, cols_in), (rows_ref, rows_in), (front_ref.at[TILE:, TILE:], front_in)], sems
    )
    solve_panels(where_ref[0], copies, cols_in, rows_in, factor_ref, TILE, xs, cs, rs, ls, ts)
    factor_ref[:TILE, :] = lower_ref[...]
    copies[4].wait()
    for begin, width in chunks(front_in.shape[1]):
        here = slice(begin, begin + width)
        left = (ls[0][...], ls[1][...])
        schur = front_in[:, here] - dot3(left, (ts[0][:, here], ts[1][:, here]), ((1,), (0,)))
        for b in range(begin // TILE, (begin + width) // TILE):
            at = slice(b * TILE - begin, (b + 1) * TILE - begin)
            for a in range(STEPS - 1):
                slot = where_ref[1 + a] * STEPS + where_ref[STEPS + b]
                box_ref[slot] = schur[a * TILE : (a + 1) * TILE, at]


def panel_scratch(rows, cols, gathered):
    given = [(STEPS, rows, TILE), gathered, (rows, cols)]
    pairs = [(ORDER, ORDER), (rows, ORDER), (ORDER, cols), (rows, ORDER), (ORDER, cols)]
    return (
        [pltpu.VMEM(shape, jnp.float32) for shape in given]
        + [pltpu.SemaphoreType.DMA((5,))]
        + [pltpu.VMEM(shape, jnp.bfloat16) for shape in pairs for _ in range(2)]
    )


def child_update(where, front, cols, rows, x, lower):
    kept = front.shape[0] - TILE, front.shape[1] - TILE
    return pl.pallas_call(
        child_kernel,
        out_shape=(
            jax.ShapeDtypeStruct((STEPS * STEPS, TILE, TILE), jnp.float32),
            jax.ShapeDtypeStruct((front.shape[0], TILE), jnp.float32),
        ),
        in_specs=[SMEM] + [ANY] * 5 + [VMEM],
        out_specs=(VMEM, VMEM),
        scratch_shapes=panel_scratch(*kept, rows.shape),
        compiler_params=pltpu.CompilerParams(vmem_limit_bytes=58 << 20),
        name="child_update",
    )(where, front, cols, rows, *x, lower)


def parent_kernel(where_ref, front_ref, cols_ref, rows_ref, x_high_ref, x_rest_ref, lower_ref, out_ref, factor_ref, *scratch):
    cols_in, rows_in, front_in, sems = scratch[:4]
    xs, cs, rs, ls, ts = (scratch[i : i + 2] for i in range(4, 14, 2))
    col, core = where_ref[0], where_ref[1]
    copies = fetch([(x_high_ref, xs[0]), (x_rest_ref, xs[1]), (cols_ref, cols_in), (rows_ref, rows_in), (front_ref.at[:, TILE:], front_in)], sems)
    solve_panels(col, copies, cols_in, rows_in, factor_ref, 0, xs, cs, rs, ls, ts)

    @pl.when(core == 0)
    def _():
        factor_ref[:TILE, :] = lower_ref[...]

    copies[4].wait()
    out_ref[:, :TILE] = jnp.zeros((front_in.shape[0], TILE), jnp.float32)
    for begin, width in chunks(front_in.shape[1]):
        here = slice(begin, begin + width)
        left = (ls[0][...], ls[1][...])
        out_ref[:, TILE + begin : TILE + begin + width] = front_in[:, here] - dot3(
            left, (ts[0][:, here], ts[1][:, here]), ((1,), (0,))
        )

    @pl.when(core == 0)
    def _():
        out_ref[:TILE, :] = jnp.zeros((TILE, out_ref.shape[1]), jnp.float32)


def parent_update(where, front, cols, rows, x, lower):
    return pl.pallas_call(
        parent_kernel,
        out_shape=(
            jax.ShapeDtypeStruct(front.shape, jnp.float32),
            jax.ShapeDtypeStruct((front.shape[0], TILE), jnp.float32),
        ),
        in_specs=[SMEM] + [ANY] * 5 + [VMEM],
        out_specs=(VMEM, VMEM),
        scratch_shapes=panel_scratch(front.shape[0], front.shape[1] - TILE, rows.shape),
        compiler_params=pltpu.CompilerParams(vmem_limit_bytes=60 << 20),
        name="parent_update",
    )(where, front, cols, rows, *x, lower)


def assemble_kernel(rows_ref, cols_ref, front_ref, own_ref, other_ref, result_ref, out_ref, sems):
    tiles_row, tiles_col = (n // TILE for n in front_ref.shape)
    out_ref[...] = front_ref[...]
    def add_row(child, i, at):
        source = rows_ref[child * tiles_row + i]

        def add(box_ref, base):
            for j in range(tiles_col):
                place = cols_ref[child * tiles_col + j]

                @pl.when(place >= 0)
                def _():
                    out_ref[at, j * TILE : (j + 1) * TILE] += box_ref[base + place]

        @pl.when((source >= 0) & (source < STEPS * STEPS))
        def _():
            add(own_ref, source)

        @pl.when(source >= STEPS * STEPS)
        def _():
            add(other_ref, source - STEPS * STEPS)

    copies = []
    for i in range(tiles_row):
        at = slice(i * TILE, (i + 1) * TILE)
        for child in range(2):
            add_row(child, i, at)
        copies.append(pltpu.make_async_copy(out_ref.at[at], result_ref.at[at], sems.at[i]))
        copies[-1].start()
    for copy in copies:
        copy.wait()


def assemble(rows, cols, front, own, other):
    return pl.pallas_call(
        assemble_kernel,
        out_shape=jax.ShapeDtypeStruct(front.shape, jnp.float32),
        in_specs=[SMEM, SMEM] + [VMEM] * 3,
        out_specs=HBM,
        scratch_shapes=[pltpu.VMEM(front.shape, jnp.float32), pltpu.SemaphoreType.DMA((front.shape[0] // TILE,))],
        compiler_params=pltpu.CompilerParams(vmem_limit_bytes=60 << 20),
        name="assemble",
    )(rows, cols, front, own, other)


def spread(x, axes, first=None):
    count = lax.axis_size(axes)
    copies = jnp.broadcast_to(x[None], (count,) + x.shape)
    if first is not None:
        copies = after(copies, first)
    return lax.all_to_all(copies, axes, 0, 0, tiled=True)


def after(x, first):
    return lax.optimization_barrier((x, first))[0]


def local(child_fronts, child_map, parent_front):
    child = lax.axis_index("sub")
    core = lax.axis_index("core")
    row = lax.axis_index(("y", "core"))
    col = lax.axis_index(COL)
    group = lax.axis_index(GROUP)
    front = child_fronts[0]
    kept = CBLK // STEPS - 1

    piece = pack(front[:TILE, :TILE], row, col)[:72]
    own = spread(piece, ("y",) + COL).reshape((-1, STEPS) + piece.shape)
    rows = lax.all_gather(after(front[:TILE, TILE:], own), ("y", "core"), axis=0, tiled=True)
    other = lax.ppermute(own, "core", SWAP)
    columns = spread(front[TILE:, :TILE], COL, own)
    *inverse, lower = factor(jnp.stack([core, row, col]).astype(jnp.int32), own, other)
    columns = after(columns, lower)
    mine = child_map[child] // (PBLK // STEPS)
    where = jnp.concatenate(
        [
            col.reshape(1),
            lax.dynamic_slice(mine, (row * kept,), (kept,)),
            lax.dynamic_slice(mine, (col * kept,), (kept,)),
        ]
    ).astype(jnp.int32)
    box, child_factor = child_update(where, front, columns, rows, inverse, lower)

    box = lax.all_to_all(box, GROUP + COL, 0, 0, tiled=True)
    box_other = lax.ppermute(box, "core", SWAP)
    tiles_row, tiles_col = parent_front.shape[0] // TILE, parent_front.shape[1] // TILE
    blocks = jnp.arange(PBLK, dtype=jnp.int32)
    number = jnp.arange(CBLK - STEPS, dtype=jnp.int32)
    source = jnp.max(jnp.where(child_map[:, :, None] == blocks, number[:, None], -1), axis=1)
    source_row = lax.dynamic_slice(source, (0, (2 * group + core) * tiles_row), (2, tiles_row))
    source_col = lax.dynamic_slice(source, (0, col * tiles_col), (2, tiles_col))
    whose = (source_row // kept % 2 != core).astype(jnp.int32) * (STEPS * STEPS)
    place = whose + jnp.arange(2, dtype=jnp.int32)[:, None] * (STEPS * STEPS // 2) + source_row // (2 * kept) * STEPS
    place_row = jnp.where(source_row >= 0, place, -1)
    place_col = jnp.where(source_col >= 0, source_col // kept, -1)
    front = assemble(place_row.reshape(-1), place_col.reshape(-1), parent_front, box, box_other)

    down = [(0, 1)]
    half = TILE // 2
    strip = jnp.where(core == 0, front[:half, :], lax.ppermute(front[half:TILE, :], "core", down))
    strip_other = lax.ppermute(strip[:, TILE:], "sub", SWAP)
    piece = pack(front[:TILE, :TILE], group, col)
    part = piece.shape[0] // 2
    piece = jnp.where(core == 0, piece[:part], lax.ppermute(piece[part:], "core", down))
    own = spread(piece, GROUP + COL).reshape((-1, STEPS) + piece.shape)
    other = lax.ppermute(own, "core", SWAP)
    strip_other = after(strip_other, own)
    both = jnp.stack([jnp.where(child == i, strip[:, TILE:], strip_other) for i in range(2)])
    rows = lax.all_gather(both, ("y", "core"), axis=0)
    columns = spread(front[:, :TILE], COL, own)
    *inverse, lower = factor(jnp.stack([core, group, col]).astype(jnp.int32), own, other)
    rows, columns = after((rows, columns), lower)
    where = jnp.stack([col, core]).astype(jnp.int32)
    update, parent_factor = parent_update(where, front, columns, rows, inverse, lower)
    return (child_factor[None], parent_factor, update)


def solution(mesh):
    shape = (2, 4, 2, 2, 4)
    fine = jax.sharding.Mesh(mesh.devices.reshape(shape), ("sub", "y", "core", "xlo", "z"))
    in_specs = (P("sub", ("y", "core"), COL), P(), P(("sub", "y", "core"), COL))
    out_specs = (P("sub", ("y", "core"), COL), P(("sub", "y", "core"), COL), P(("sub", "y", "core"), COL))
    return jax.shard_map(local, mesh=fine, in_specs=in_specs, out_specs=out_specs, check_vma=False)
```
